32 devices in a mesh: blk: 8 (over z, y), group: 4 (over x, core).
Axes of the slice: x: 2, y: 2, z: 4, core: 2. Of those that a mesh axis runs over, the one named last changes fastest.
Arguments:
- expression: bfloat16 [12288, 2048], P(('blk', 'group')), may hold values from -6 to 6
- observed: int32 [12288, 2048], P(('blk', 'group')), may hold values 0 or 1
- cell_factors: float32 [12288, 512], P(('blk', 'group')), may hold values from -1.2613447 to 1.2613447
- locus_factors: float32 [2048, 512], P('blk'), may hold values from -1.2613447 to 1.2613447
Outputs:
- cells_out: float32 [12288, 512], P(('blk', 'group'))
- loci_out: float32 [2048, 512], P('blk')
The draws below stay inside these ranges and needn't reach their ends.
All inputs are finite; a program needn't handle non-finite values. No bound on the sum of `observed` on one device may be relied on, other than what follows from the above.
Results may differ from the reference program's by a relative error of at most 0.00095.
Values sent between devices are 32-bit elements; how exact they have to be, the bound alone decides.
No kernel may reach another device: no remote copies, remote signals or barrier semaphores. Data moves between devices by JAX's collectives and lax.ppermute only.
A program may use at most 64 MiB of HBM per device.

```python
import jax
import jax.numpy as jnp
from jax import lax

R = 512
LOC_BLK = 256
CELL_DEV = 384
HOPS = 6
SWEEPS = 2
CELLS = 12288
LOCI = 2048
N_BLK = 8
N_GROUP = 4


def with_ends(values, rng, low, top_value):
    longest = values.shape.index(max(values.shape))
    spots = []
    for shift in (0, 1):
        where = [jax.random.randint(jax.random.fold_in(rng, axis), (), 0, length) for axis, length in enumerate(values.shape)]
        where[longest] = (where[longest] + shift) % values.shape[longest]
        spots.append(tuple(where))
    return values.at[spots[0]].set(low).at[spots[1]].set(top_value)


def level_of(stream_key, extent, split, smallest, top_value):
    def one(dim, blocks):
        heights = jax.random.uniform(jax.random.fold_in(jax.random.fold_in(stream_key, 6), dim), (blocks,), jnp.float32, smallest / len(split), top_value / len(split))
        return jnp.repeat(jnp.exp(heights), extent[dim] // blocks).reshape((-1,) + (1,) * (len(extent) - dim - 1))

    factor_of = one(*split[0])
    for cut in split[1:]:
        factor_of = factor_of * one(*cut)
    return factor_of


def gaussian(rng, shape, deviation, bound, pieces=(), kind=jnp.bfloat16):
    level = level_of(rng, shape, pieces, -0.22, 0.18) if pieces else 1.0
    result = jax.random.normal(rng, shape, jnp.float32) * deviation * level
    return jnp.minimum(jnp.maximum(result, -bound), bound).astype(kind)


def setup_inputs(seed: int = 0) -> dict:
    seeds = jax.random.split(jax.random.key(seed), 5)
    return {
        "expression": gaussian(seeds[0], (CELLS, LOCI), 1.0, 6.0, ((0, 32),)),
        "observed": with_ends((jax.random.randint(seeds[1], (CELLS, LOCI), 0, 2) < 1).astype(jnp.int32), jax.random.fold_in(seeds[1], 1), 0, 1),
        "cell_factors": gaussian(seeds[2], (CELLS, R), (R ** -0.25), 1.2613447, ((0, 32),), jnp.float32),
        "locus_factors": gaussian(seeds[3], (LOCI, R), (R ** -0.25), 1.2613447, ((0, 8),), jnp.float32),
    }


def sweep(cell_rows, locus_rows, tile_data, weights):
    cell_half = cell_rows.astype(jnp.bfloat16)
    locus_half = locus_rows.astype(jnp.bfloat16)
    predicted = lax.dot_general(cell_half, locus_half, (((1,), (1,)), ((), ())), preferred_element_type=jnp.float32)
    residue = (weights * (tile_data.astype(jnp.float32) - predicted)).astype(jnp.bfloat16)
    grad_cells = jnp.dot(residue, locus_half, preferred_element_type=jnp.float32)
    grad_locus = lax.dot_general(residue, cell_half, (((0,), (0,)), ((), ())), preferred_element_type=jnp.float32)
    rank_width = cell_rows.shape[1]
    cell_step = 2.0 / (locus_rows.shape[0] + rank_width)
    locus_step = 2.0 / (cell_rows.shape[0] + rank_width)
    return cell_rows + cell_step * grad_cells, locus_rows + locus_step * grad_locus


def visit_device(cell_rows, locus_rows, tile_data, mask_tile):
    weights = mask_tile.astype(jnp.float32)
    for sweep_index in range(SWEEPS):
        cell_rows, locus_rows = sweep(cell_rows, locus_rows, tile_data, weights)
    return cell_rows, locus_rows


def visit_column(packed):
    cell_rows, locus_rows, tile_data, mask_tile = packed
    return jax.vmap(visit_device)(cell_rows, locus_rows, tile_data, mask_tile)


def reference(expression, observed, cell_factors, locus_factors):
    cycle_size = N_BLK
    group_size = N_GROUP
    expr_cube = expression.reshape(cycle_size, group_size, CELL_DEV, cycle_size, LOC_BLK)
    mask_cube = observed.reshape(cycle_size, group_size, CELL_DEV, cycle_size, LOC_BLK)
    cell_rows = cell_factors.reshape(cycle_size, group_size, CELL_DEV, R)
    held = jnp.broadcast_to(locus_factors.reshape(cycle_size, 1, LOC_BLK, R), (cycle_size, group_size, LOC_BLK, R))
    cycle_rows = jnp.arange(cycle_size, dtype=jnp.int32)
    for hop_index in range(HOPS):
        held_blocks = ((cycle_rows - hop_index) % cycle_size).astype(jnp.int32)
        tiles = expr_cube[cycle_rows, :, :, held_blocks]
        masks = mask_cube[cycle_rows, :, :, held_blocks]
        cell_rows, held = lax.map(visit_column, (cell_rows, held, tiles, masks))
        if hop_index == HOPS // 2 - 1 or hop_index == HOPS - 1:
            averaged = jnp.sum(held, axis=1, keepdims=True) / group_size
            held = jnp.broadcast_to(averaged, held.shape)
        if hop_index < HOPS - 1:
            held = jnp.roll(held, 1, axis=0)
    held = jnp.roll(held, 1 - HOPS, axis=0)
    return cell_rows.reshape(CELLS, R), held[:, 0].reshape(LOCI, R)
```

```python
import jax
import jax.numpy as jnp
from jax import lax
from jax.sharding import PartitionSpec as P

HOPS = 6
SWEEPS = 2
CHUNKS = 2
AXES = ("blk", "group")


def moved(block, blocks, groups, distance, flip=0):
    route = [
        (b * groups + g, (b + distance) % blocks * groups + (g ^ flip))
        for b in range(blocks)
        for g in range(groups)
    ]
    return lax.ppermute(block, AXES, route)


def halves(block):
    rows = block.shape[0] // 2
    return block[:rows], block[rows:]


def average(locus_rows, blocks, groups, distance):
    member = lax.axis_index("group")
    bits = [1 << i for i in range(groups.bit_length() - 1)]
    share = locus_rows
    for bit in bits:
        low, high = halves(share)
        upper = (member & bit) != 0
        share = jnp.where(upper, high, low) + moved(jnp.where(upper, low, high), blocks, groups, 0, bit)
    share = share / groups
    for place, bit in enumerate(reversed(bits)):
        upper = (member & bit) != 0
        if place == 0:
            mine = moved(share, blocks, groups, distance)
            other = moved(share, blocks, groups, distance, bit)
        else:
            mine = share
            other = moved(share, blocks, groups, 0, bit)
        share = jnp.where(
            upper, jnp.concatenate([other, mine], 0), jnp.concatenate([mine, other], 0)
        )
    return share


def visit(cell_rows, parts, tiles, masks):
    rank_width = cell_rows.shape[1]
    cell_step = 2.0 / (sum(p.shape[0] for p in parts) + rank_width)
    locus_step = 2.0 / (cell_rows.shape[0] + rank_width)
    for _ in range(SWEEPS):
        cell_half = cell_rows.astype(jnp.bfloat16)
        grad_cells = None
        updated = []
        for part, tile, mask in zip(parts, tiles, masks):
            half = part.astype(jnp.bfloat16)
            predicted = lax.dot_general(
                cell_half, half, (((1,), (1,)), ((), ())), preferred_element_type=jnp.float32
            )
            residue = (mask * (tile - predicted)).astype(jnp.bfloat16)
            term = jnp.dot(residue, half, preferred_element_type=jnp.float32)
            grad_cells = term if grad_cells is None else grad_cells + term
            grad_locus = lax.dot_general(
                residue, cell_half, (((0,), (0,)), ((), ())), preferred_element_type=jnp.float32
            )
            updated.append(part + locus_step * grad_locus)
        cell_rows = cell_rows + cell_step * grad_cells
        parts = updated
    return cell_rows, parts


def solution(mesh):
    blocks, groups = mesh.shape["blk"], mesh.shape["group"]

    def on_device(expression, observed, cell_factors, locus_factors):
        position = lax.axis_index("blk")
        block_rows = locus_factors.shape[0]
        size = block_rows // CHUNKS
        cell_rows = cell_factors
        parts = [locus_factors[c * size : (c + 1) * size] for c in range(CHUNKS)]
        for hop in range(HOPS):
            offset = (position - hop) % blocks * block_rows
            tiles = [
                lax.dynamic_slice_in_dim(expression, offset + c * size, size, 1).astype(jnp.float32)
                for c in range(CHUNKS)
            ]
            masks = [
                lax.dynamic_slice_in_dim(observed, offset + c * size, size, 1).astype(jnp.float32)
                for c in range(CHUNKS)
            ]
            cell_rows, parts = visit(cell_rows, parts, tiles, masks)
            if hop == HOPS // 2 - 1 or hop == HOPS - 1:
                distance = 1 if hop < HOPS - 1 else 1 - HOPS
                whole = average(jnp.concatenate(parts, 0), blocks, groups, distance)
                parts = [whole[c * size : (c + 1) * size] for c in range(CHUNKS)]
            else:
                parts = [moved(p, blocks, groups, 1) for p in parts]
        return cell_rows, jnp.concatenate(parts, 0)

    split = P(AXES, None)
    return jax.shard_map(
        on_device,
        mesh=mesh,
        in_specs=(split, split, split, P("blk", None)),
        out_specs=(split, P("blk", None)),
        check_vma=False,
    )
```

```python
import functools

import jax
import jax.numpy as jnp
from jax import lax
from jax.experimental import pallas as pl
from jax.experimental.pallas import tpu as pltpu
from jax.sharding import PartitionSpec as P

HOPS = 6
AXES = ("blk", "group")
F32, HALF = jnp.float32, jnp.bfloat16


def across(a, b):
    return lax.dot_general(a, b, (((1,), (1,)), ((), ())), preferred_element_type=F32)


def along(a, b):
    return lax.dot_general(a, b, (((0,), (0,)), ((), ())), preferred_element_type=F32)


def times(a, b):
    return jnp.dot(a, b, preferred_element_type=F32)


def residue(x_ref, m_ref, cell_half, locus_half):
    difference = x_ref[...].astype(F32) - across(cell_half, locus_half)
    return (m_ref[...].astype(F32) * difference).astype(HALF)


def tile_copies(first, x_hbm, m_hbm, xa, ma, xb, mb, sems):
    width = xa.shape[1]
    copies = []
    for place, (x_out, m_out) in enumerate(((xa, ma), (xb, mb))):
        column = first if place == 0 else first + 1 - 2 * (first % 2)
        columns = pl.ds(pl.multiple_of(column * width, width), width)
        copies.append(pltpu.make_async_copy(x_hbm.at[:, columns], x_out, sems.at[2 * place]))
        copies.append(pltpu.make_async_copy(m_hbm.at[:, columns], m_out, sems.at[2 * place + 1]))
    return copies


def load_body(first, x_hbm, m_hbm, u_hbm, v_hbm, xa, ma, xb, mb, u, va, vb, sems):
    rows = va.shape[0]
    half = first[0] % 2
    copies = tile_copies(first[0], x_hbm, m_hbm, xa, ma, xb, mb, sems)
    copies.append(pltpu.make_async_copy(u_hbm, u, sems.at[4]))
    for place, (out, index) in enumerate(((va, half), (vb, 1 - half))):
        at = pl.ds(pl.multiple_of(index * rows, rows), rows)
        copies.append(pltpu.make_async_copy(v_hbm.at[at], out, sems.at[5 + place]))
    for copy in copies:
        copy.start()
    for copy in copies:
        copy.wait()


def open_body(steps, u, va, xa, ma, grad_u, va1):
    cell_half, locus_half = u[...].astype(HALF), va[...].astype(HALF)
    r = residue(xa, ma, cell_half, locus_half)
    grad_u[...] = times(r, locus_half)
    va1[...] = va[...] + steps[1] * along(r, cell_half)


def turn_body(steps, u, grad_u, va1, vb, xa, ma, xb, mb, u1, va2, r1b, r2a):
    cell_half, locus_half = u[...].astype(HALF), vb[...].astype(HALF)
    r = residue(xb, mb, cell_half, locus_half)
    r1b[...] = r
    moved_u = u[...] + steps[0] * (grad_u[...] + times(r, locus_half))
    u1[...] = moved_u
    cell_half, locus_half = moved_u.astype(HALF), va1[...].astype(HALF)
    r = residue(xa, ma, cell_half, locus_half)
    r2a[...] = r
    va2[...] = va1[...] + steps[1] * along(r, cell_half)


def close_body(
    steps, first, u, u1, r1b, r2a, va1, vb, xb, mb, x_hbm, m_hbm,
    vb2, u2, xa_next, ma_next, xb_next, mb_next, sems,
):
    copies = tile_copies(first[0], x_hbm, m_hbm, xa_next, ma_next, xb_next, mb_next, sems)
    for copy in copies:
        copy.start()
    vb1 = vb[...] + steps[1] * along(r1b[...], u[...].astype(HALF))
    cell_half, locus_half = u1[...].astype(HALF), vb1.astype(HALF)
    r = residue(xb, mb, cell_half, locus_half)
    vb2[...] = vb1 + steps[1] * along(r, cell_half)
    u2[...] = u1[...] + steps[0] * (times(r2a[...], va1[...].astype(HALF)) + times(r, locus_half))
    for copy in copies:
        copy.wait()


def call(body, args, spaces, outs, sems=0, flops=0):
    kinds = {"v": pltpu.VMEM, "h": pl.ANY, "s": pltpu.SMEM}
    pinned = [
        pltpu.with_memory_space_constraint(a, pltpu.VMEM) if s == "v" else a
        for a, s in zip(args, spaces)
    ]
    moved_bytes = sum(a.size * a.dtype.itemsize for a in args) if sems == 0 else 4 << 20
    return pl.pallas_call(
        body,
        out_shape=[pltpu.VMEM(shape, dtype) for shape, dtype in outs],
        in_specs=[pl.BlockSpec(memory_space=kinds[s]) for s in spaces],
        out_specs=[pl.BlockSpec(memory_space=pltpu.VMEM) for _ in outs],
        scratch_shapes=[pltpu.SemaphoreType.DMA((sems,))] if sems else [],
        compiler_params=pltpu.CompilerParams(vmem_limit_bytes=24 << 20),
        cost_estimate=pl.CostEstimate(flops=flops, bytes_accessed=moved_bytes, transcendentals=0),
    )(*pinned)


def moved(block, blocks, groups, distance, flip=0):
    route = [
        (b * groups + g, (b + distance) % blocks * groups + (g ^ flip))
        for b in range(blocks)
        for g in range(groups)
    ]
    return lax.ppermute(block, AXES, route)


def average(part_a, part_b, blocks, groups, distance):
    member = lax.axis_index("group")
    bits = [1 << i for i in range(1, groups.bit_length() - 1)]
    share = part_a + moved(part_b, blocks, groups, 0, 1)
    for bit in bits:
        rows = share.shape[0] // 2
        upper = (member & bit) != 0
        low, high = share[:rows], share[rows:]
        share = jnp.where(upper, high, low) + moved(jnp.where(upper, low, high), blocks, groups, 0, bit)
    share = share / groups
    for place, bit in enumerate(reversed(bits)):
        upper = (member & bit) != 0
        if place == 0:
            mine = moved(share, blocks, groups, distance)
            other = moved(share, blocks, groups, distance, bit)
        else:
            mine = share
            other = moved(share, blocks, groups, 0, bit)
        share = jnp.where(
            upper, jnp.concatenate([other, mine], 0), jnp.concatenate([mine, other], 0)
        )
    return share, moved(share, blocks, groups, 0, 1)


def solution(mesh):
    blocks, groups = mesh.shape["blk"], mesh.shape["group"]

    def on_device(expression, observed, cell_factors, locus_factors):
        position = lax.axis_index("blk")
        side = lax.axis_index("group") % 2
        cells, rank = cell_factors.shape
        rows = locus_factors.shape[0] // 2
        steps = (2.0 / (2 * rows + rank), 2.0 / (cells + rank))
        wide, tall = ((cells, rank), F32), ((rows, rank), F32)
        tiles = [((cells, rows), HALF), ((cells, rows), jnp.int32)] * 2
        small = ((cells, rows), HALF)
        work = 2 * cells * rows * rank

        def first(hop):
            return ((position - hop) % blocks * 2 + side).reshape(1).astype(jnp.int32)

        xa, ma, xb, mb, u, va, vb = call(
            load_body,
            (first(0), expression, observed, cell_factors, locus_factors),
            "shhhh",
            tiles + [wide, tall, tall],
            7,
        )
        for hop in range(HOPS):
            grad_u, va1 = call(
                functools.partial(open_body, steps), (u, va, xa, ma), "vvvv", [wide, tall], 0, 3 * work
            )
            u1, va2, r1b, r2a = call(
                functools.partial(turn_body, steps),
                (u, grad_u, va1, vb, xa, ma, xb, mb),
                "vvvvvvvv",
                [wide, tall, small, small],
                0,
                4 * work,
            )
            vb2, u, xa, ma, xb, mb = call(
                functools.partial(close_body, steps),
                (first(hop + 1), u, u1, r1b, r2a, va1, vb, xb, mb, expression, observed),
                "svvvvvvvvhh",
                [tall, wide] + tiles,
                4,
                5 * work,
            )
            if hop == HOPS // 2 - 1 or hop == HOPS - 1:
                distance = 1 if hop < HOPS - 1 else 1 - HOPS
                va, vb = average(va2, vb2, blocks, groups, distance)
            else:
                va, vb = (moved(part, blocks, groups, 1) for part in (va2, vb2))
        whole = jnp.where(side == 0, jnp.concatenate([va, vb], 0), jnp.concatenate([vb, va], 0))
        return u, whole

    split = P(AXES, None)
    return jax.shard_map(
        on_device,
        mesh=mesh,
        in_specs=(split, split, split, P("blk", None)),
        out_specs=(split, P("blk", None)),
        check_vma=False,
    )
```

```python
import functools

import jax
import jax.numpy as jnp
from jax import lax
from jax.experimental import pallas as pl
from jax.experimental.pallas import tpu as pltpu
from jax.sharding import PartitionSpec as P

HOPS = 6
AXES = ("blk", "group")
F32, HALF = jnp.float32, jnp.bfloat16


def across(a, b):
    return lax.dot_general(a, b, (((1,), (1,)), ((), ())), preferred_element_type=F32)


def along(a, b):
    return lax.dot_general(a, b, (((0,), (0,)), ((), ())), preferred_element_type=F32)


def times(a, b):
    return jnp.dot(a, b, preferred_element_type=F32)


def residue(tile, mask, place, cell_half, locus_half):
    width = locus_half.shape[0]
    columns = slice(place * width, (place + 1) * width)
    difference = tile[:, columns].astype(F32) - across(cell_half, locus_half)
    return (mask[:, columns].astype(F32) * difference).astype(HALF)


def tile_copies(first, x_hbm, m_hbm, tile, mask, sems):
    width = tile.shape[1] // 2
    copies = []
    for place, column in enumerate((first, first + 1 - 2 * (first % 2))):
        source = pl.ds(pl.multiple_of(column * width, width), width)
        target = pl.ds(place * width, width)
        for i, (whole, part) in enumerate(((x_hbm, tile), (m_hbm, mask))):
            copies.append(
                pltpu.make_async_copy(whole.at[:, source], part.at[:, target], sems.at[2 * place + i])
            )
    return copies


def load_body(first, x_hbm, m_hbm, u_hbm, v_hbm, tile, mask, u, va, vb, sems):
    rows = va.shape[0]
    half = first[0] % 2
    copies = tile_copies(first[0], x_hbm, m_hbm, tile, mask, sems)
    copies.append(pltpu.make_async_copy(u_hbm, u, sems.at[4]))
    for place, (out, index) in enumerate(((va, half), (vb, 1 - half))):
        at = pl.ds(pl.multiple_of(index * rows, rows), rows)
        copies.append(pltpu.make_async_copy(v_hbm.at[at], out, sems.at[5 + place]))
    for copy in copies:
        copy.start()
    for copy in copies:
        copy.wait()


def open_body(steps, u, va, tile, mask, grad_u, va1):
    cell_half, locus_half = u[...].astype(HALF), va[...].astype(HALF)
    r = residue(tile, mask, 0, cell_half, locus_half)
    grad_u[...] = times(r, locus_half)
    va1[...] = va[...] + steps[1] * along(r, cell_half)


def turn_body(steps, u, grad_u, va1, vb, tile, mask, u1, va2, rest):
    width = vb.shape[0]
    cell_half, locus_half = u[...].astype(HALF), vb[...].astype(HALF)
    r = residue(tile, mask, 1, cell_half, locus_half)
    rest[:, width:] = r
    moved_u = u[...] + steps[0] * (grad_u[...] + times(r, locus_half))
    u1[...] = moved_u
    cell_half, locus_half = moved_u.astype(HALF), va1[...].astype(HALF)
    r = residue(tile, mask, 0, cell_half, locus_half)
    rest[:, :width] = r
    va2[...] = va1[...] + steps[1] * along(r, cell_half)


def close_body(
    steps, first, u, u1, rest, va1, vb, tile, mask, x_hbm, m_hbm, vb2, u2, tile_next, mask_next, sems
):
    width = vb.shape[0]
    copies = tile_copies(first[0], x_hbm, m_hbm, tile_next, mask_next, sems)
    for copy in copies:
        copy.start()
    vb1 = vb[...] + steps[1] * along(rest[:, width:], u[...].astype(HALF))
    cell_half, locus_half = u1[...].astype(HALF), vb1.astype(HALF)
    r = residue(tile, mask, 1, cell_half, locus_half)
    vb2[...] = vb1 + steps[1] * along(r, cell_half)
    grad_u = times(rest[:, :width], va1[...].astype(HALF)) + times(r, locus_half)
    u2[...] = u1[...] + steps[0] * grad_u
    for copy in copies:
        copy.wait()


def call(body, args, spaces, outs, sems=0, flops=0):
    kinds = {"v": pltpu.VMEM, "h": pltpu.HBM, "s": pltpu.SMEM}
    pinned = [
        a if s == "s" else pltpu.with_memory_space_constraint(a, kinds[s])
        for a, s in zip(args, spaces)
    ]
    moved_bytes = sum(a.size * a.dtype.itemsize for a in args) if sems == 0 else 4 << 20
    return pl.pallas_call(
        body,
        out_shape=[jax.ShapeDtypeStruct(shape, dtype) for shape, dtype in outs],
        in_specs=[pl.BlockSpec(memory_space=kinds[s]) for s in spaces],
        out_specs=[pl.BlockSpec(memory_space=pltpu.VMEM) for _ in outs],
        scratch_shapes=[pltpu.SemaphoreType.DMA((sems,))] if sems else [],
        compiler_params=pltpu.CompilerParams(vmem_limit_bytes=8 << 20),
        cost_estimate=pl.CostEstimate(flops=flops, bytes_accessed=moved_bytes, transcendentals=0),
    )(*pinned)


def moved(block, blocks, groups, distance, flip=0):
    route = [
        (b * groups + g, (b + distance) % blocks * groups + (g ^ flip))
        for b in range(blocks)
        for g in range(groups)
    ]
    return lax.ppermute(block, AXES, route)


def average(part_a, part_b, blocks, groups, distance):
    member = lax.axis_index("group")
    bits = [1 << i for i in range(1, groups.bit_length() - 1)]
    share = part_a + moved(part_b, blocks, groups, 0, 1)
    for bit in bits:
        rows = share.shape[0] // 2
        upper = (member & bit) != 0
        low, high = share[:rows], share[rows:]
        share = jnp.where(upper, high, low) + moved(jnp.where(upper, low, high), blocks, groups, 0, bit)
    share = share / groups
    for place, bit in enumerate(reversed(bits)):
        upper = (member & bit) != 0
        if place == 0:
            mine = moved(share, blocks, groups, distance)
            other = moved(share, blocks, groups, distance, bit)
        else:
            mine = share
            other = moved(share, blocks, groups, 0, bit)
        share = jnp.where(
            upper, jnp.concatenate([other, mine], 0), jnp.concatenate([mine, other], 0)
        )
    return share, moved(share, blocks, groups, 0, 1)


def solution(mesh):
    blocks, groups = mesh.shape["blk"], mesh.shape["group"]

    def on_device(expression, observed, cell_factors, locus_factors):
        position = lax.axis_index("blk")
        side = lax.axis_index("group") % 2
        cells, rank = cell_factors.shape
        rows = locus_factors.shape[0] // 2
        steps = (2.0 / (2 * rows + rank), 2.0 / (cells + rank))
        wide, tall = ((cells, rank), F32), ((rows, rank), F32)
        tiles = [((cells, 2 * rows), HALF), ((cells, 2 * rows), jnp.int32)]
        work = 2 * cells * rows * rank

        def first(hop):
            return ((position - hop) % blocks * 2 + side).reshape(1).astype(jnp.int32)

        tile, mask, u, va, vb = call(
            load_body,
            (first(0), expression, observed, cell_factors, locus_factors),
            "shhhh",
            tiles + [wide, tall, tall],
            7,
        )
        for hop in range(HOPS):
            grad_u, va1 = call(
                functools.partial(open_body, steps), (u, va, tile, mask), "vvvv", [wide, tall], 0, 3 * work
            )
            u1, va2, rest = call(
                functools.partial(turn_body, steps),
                (u, grad_u, va1, vb, tile, mask),
                "vvvvvv",
                [wide, tall, ((cells, 2 * rows), HALF)],
                0,
                4 * work,
            )
            vb2, u, tile, mask = call(
                functools.partial(close_body, steps),
                (first(hop + 1), u, u1, rest, va1, vb, tile, mask, expression, observed),
                "svvvvvvvhh",
                [tall, wide] + tiles,
                4,
                5 * work,
            )
            if hop == HOPS // 2 - 1 or hop == HOPS - 1:
                distance = 1 if hop < HOPS - 1 else 1 - HOPS
                va, vb = average(va2, vb2, blocks, groups, distance)
            else:
                va, vb = (moved(part, blocks, groups, 1) for part in (va2, vb2))
        whole = jnp.where(side == 0, jnp.concatenate([va, vb], 0), jnp.concatenate([vb, va], 0))
        return u, whole

    split = P(AXES, None)
    return jax.shard_map(
        on_device,
        mesh=mesh,
        in_specs=(split, split, split, P("blk", None)),
        out_specs=(split, P("blk", None)),
        check_vma=False,
    )
```

```python
import functools

import jax
import jax.numpy as jnp
from jax import lax
from jax.experimental import pallas as pl
from jax.experimental.pallas import tpu as pltpu
from jax.sharding import PartitionSpec as P

HOPS = 6
AXES = ("blk", "group")
F32, HALF = jnp.float32, jnp.bfloat16


def across(a, b):
    return lax.dot_general(a, b, (((1,), (1,)), ((), ())), preferred_element_type=F32)


def along(a, b):
    return lax.dot_general(a, b, (((0,), (0,)), ((), ())), preferred_element_type=F32)


def times(a, b):
    return jnp.dot(a, b, preferred_element_type=F32)


def residue(tile, mask, place, cell_half, locus_half):
    width = locus_half.shape[0]
    columns = slice(place * width, (place + 1) * width)
    difference = tile[:, columns].astype(F32) - across(cell_half, locus_half)
    return (mask[:, columns].astype(F32) * difference).astype(HALF)


def tile_copies(first, x_hbm, m_hbm, tile, mask, sems):
    width = tile.shape[1] // 2
    copies = []
    for place, column in enumerate((first, first + 1 - 2 * (first % 2))):
        source = pl.ds(pl.multiple_of(column * width, width), width)
        target = pl.ds(place * width, width)
        for i, (whole, part) in enumerate(((x_hbm, tile), (m_hbm, mask))):
            copies.append(
                pltpu.make_async_copy(whole.at[:, source], part.at[:, target], sems.at[2 * place + i])
            )
    return copies


def first_columns(place, blocks, hop, flip):
    block = lax.rem(place[0] + (blocks * HOPS - hop), blocks)
    side = 1 - place[1] if flip else place[1]
    return 2 * block + side


def load_body(blocks, place, x_hbm, m_hbm, u_hbm, v_hbm, tile, mask, u, va, vb, sems):
    rows = va.shape[0]
    half = place[1]
    copies = tile_copies(first_columns(place, blocks, 0, False), x_hbm, m_hbm, tile, mask, sems)
    copies.append(pltpu.make_async_copy(u_hbm, u, sems.at[4]))
    for order, (out, index) in enumerate(((va, half), (vb, 1 - half))):
        at = pl.ds(pl.multiple_of(index * rows, rows), rows)
        copies.append(pltpu.make_async_copy(v_hbm.at[at], out, sems.at[5 + order]))
    for copy in copies:
        copy.start()
    for copy in copies:
        copy.wait()


def open_body(steps, u, va, tile, mask, grad_u, va1):
    cell_half, locus_half = u[...].astype(HALF), va[...].astype(HALF)
    r = residue(tile, mask, 0, cell_half, locus_half)
    grad_u[...] = times(r, locus_half)
    va1[...] = va[...] + steps[1] * along(r, cell_half)


def turn_body(steps, u, grad_u, va1, vb, tile, mask, u1, va2, rest):
    width = vb.shape[0]
    cell_half, locus_half = u[...].astype(HALF), vb[...].astype(HALF)
    r = residue(tile, mask, 1, cell_half, locus_half)
    rest[:, width:] = r
    moved_u = u[...] + steps[0] * (grad_u[...] + times(r, locus_half))
    u1[...] = moved_u
    cell_half, locus_half = moved_u.astype(HALF), va1[...].astype(HALF)
    r = residue(tile, mask, 0, cell_half, locus_half)
    rest[:, :width] = r
    va2[...] = va1[...] + steps[1] * along(r, cell_half)


def close_body(steps, u, u1, rest, vb, tile, mask, vb2, vb1_half, r2b):
    width = vb.shape[0]
    vb1 = vb[...] + steps[1] * along(rest[:, width:], u[...].astype(HALF))
    cell_half, locus_half = u1[...].astype(HALF), vb1.astype(HALF)
    r = residue(tile, mask, 1, cell_half, locus_half)
    vb2[...] = vb1 + steps[1] * along(r, cell_half)
    vb1_half[...] = locus_half
    r2b[...] = r


def settle(steps, u1, rest, va1, vb1_half, r2b, u2):
    width = r2b.shape[1]
    grad_u = times(rest[:, :width], va1[...].astype(HALF)) + times(r2b[...], vb1_half[...])
    u2[...] = u1[...] + steps[0] * grad_u


def settle_body(steps, blocks, hop, flip, place, u1, rest, va1, vb1_half, r2b, x_hbm, m_hbm, u2, tile, mask, sems):
    copies = tile_copies(first_columns(place, blocks, hop, flip), x_hbm, m_hbm, tile, mask, sems)
    for copy in copies:
        copy.start()
    settle(steps, u1, rest, va1, vb1_half, r2b, u2)
    for copy in copies:
        copy.wait()


def call(body, args, spaces, outs, sems=0, flops=0):
    kinds = {"v": pltpu.VMEM, "h": pltpu.HBM, "s": pltpu.SMEM}
    pinned = [
        a if s == "s" else pltpu.with_memory_space_constraint(a, kinds[s])
        for a, s in zip(args, spaces)
    ]
    moved_bytes = sum(a.size * a.dtype.itemsize for a in args) if sems == 0 else 4 << 20
    return pl.pallas_call(
        body,
        out_shape=[jax.ShapeDtypeStruct(shape, dtype) for shape, dtype in outs],
        in_specs=[pl.BlockSpec(memory_space=kinds[s]) for s in spaces],
        out_specs=[pl.BlockSpec(memory_space=pltpu.VMEM) for _ in outs],
        scratch_shapes=[pltpu.SemaphoreType.DMA((sems,))] if sems else [],
        compiler_params=pltpu.CompilerParams(vmem_limit_bytes=8 << 20),
        cost_estimate=pl.CostEstimate(flops=flops, bytes_accessed=moved_bytes, transcendentals=0),
    )(*pinned)


def moved(block, blocks, groups, distance, flip=0):
    route = [
        (b * groups + g, (b + distance) % blocks * groups + (g ^ flip))
        for b in range(blocks)
        for g in range(groups)
    ]
    return lax.ppermute(block, AXES, route)


def average(part_a, part_b, pending, blocks, groups, distance):
    member = lax.axis_index("group")
    bits = [1 << i for i in range(1, groups.bit_length() - 1)]
    share = part_b + moved(part_a, blocks, groups, 0, 1)
    for bit in bits:
        rows = share.shape[0] // 2
        upper = (member & bit) != 0
        low, high = share[:rows], share[rows:]
        received = moved(jnp.where(upper, low, high), blocks, groups, 0, bit)
        received, *pending = lax.optimization_barrier((received, *pending))
        share = jnp.where(upper, high, low) + received
    share = share / groups
    for place, bit in enumerate(reversed(bits)):
        upper = (member & bit) != 0
        if place == 0:
            mine = moved(share, blocks, groups, distance)
            other = moved(share, blocks, groups, distance, bit)
        else:
            mine = share
            other = moved(share, blocks, groups, 0, bit)
        share = jnp.where(
            upper, jnp.concatenate([other, mine], 0), jnp.concatenate([mine, other], 0)
        )
    return share, moved(share, blocks, groups, 0, 1), pending


def solution(mesh):
    blocks, groups = mesh.shape["blk"], mesh.shape["group"]

    def on_device(expression, observed, cell_factors, locus_factors):
        position = lax.axis_index("blk")
        side = lax.axis_index("group") % 2
        cells, rank = cell_factors.shape
        rows = locus_factors.shape[0] // 2
        steps = (2.0 / (2 * rows + rank), 2.0 / (cells + rank))
        wide, tall = ((cells, rank), F32), ((rows, rank), F32)
        tiles = [((cells, 2 * rows), HALF), ((cells, 2 * rows), jnp.int32)]
        work = 2 * cells * rows * rank
        place = jnp.stack([position, side]).astype(jnp.int32)

        tile, mask, u, va, vb = call(
            functools.partial(load_body, blocks),
            (place, expression, observed, cell_factors, locus_factors),
            "shhhh",
            tiles + [wide, tall, tall],
            7,
        )
        for hop in range(HOPS):
            grad_u, va1 = call(
                functools.partial(open_body, steps), (u, va, tile, mask), "vvvv", [wide, tall], 0, 3 * work
            )
            u1, va2, rest = call(
                functools.partial(turn_body, steps),
                (u, grad_u, va1, vb, tile, mask),
                "vvvvvv",
                [wide, tall, ((cells, 2 * rows), HALF)],
                0,
                4 * work,
            )
            vb2, vb1_half, r2b = call(
                functools.partial(close_body, steps),
                (u, u1, rest, vb, tile, mask),
                "vvvvvv",
                [tall, ((rows, rank), HALF), ((cells, rows), HALF)],
                0,
                3 * work,
            )
            if hop < HOPS - 1:
                u, tile, mask = call(
                    functools.partial(settle_body, steps, blocks, hop + 1, hop + 1 >= HOPS // 2),
                    (place, u1, rest, va1, vb1_half, r2b, expression, observed),
                    "svvvvvhh",
                    [wide] + tiles,
                    4,
                    2 * work,
                )
            else:
                (u,) = call(
                    functools.partial(settle, steps), (u1, rest, va1, vb1_half, r2b), "vvvvv", [wide], 0, 2 * work
                )
            if hop == HOPS // 2 - 1 or hop == HOPS - 1:
                distance = 1 if hop < HOPS - 1 else 1 - HOPS
                va, vb, (u, tile, mask) = average(va2, vb2, (u, tile, mask), blocks, groups, distance)
            else:
                va, vb = (moved(part, blocks, groups, 1) for part in (va2, vb2))
        whole = jnp.where(side == 0, jnp.concatenate([va, vb], 0), jnp.concatenate([vb, va], 0))
        return u, whole

    split = P(AXES, None)
    return jax.shard_map(
        on_device,
        mesh=mesh,
        in_specs=(split, split, split, P("blk", None)),
        out_specs=(split, P("blk", None)),
        check_vma=False,
    )
```

```python
import functools

import jax
import jax.numpy as jnp
from jax import lax
from jax.experimental import pallas as pl
from jax.experimental.pallas import tpu as pltpu
from jax.sharding import PartitionSpec as P

HOPS = 6
AXES = ("blk", "group")
F32, HALF = jnp.float32, jnp.bfloat16


def across(a, b):
    return lax.dot_general(a, b, (((1,), (1,)), ((), ())), preferred_element_type=F32)


def along(a, b):
    return lax.dot_general(a, b, (((0,), (0,)), ((), ())), preferred_element_type=F32)


def times(a, b):
    return jnp.dot(a, b, preferred_element_type=F32)


def residue(tile, mask, place, cell_half, locus_half):
    width = locus_half.shape[0]
    columns = slice(place * width, (place + 1) * width)
    difference = tile[:, columns].astype(F32) - across(cell_half, locus_half)
    return (mask[:, columns].astype(F32) * difference).astype(HALF)


def tile_copies(first, x_hbm, m_hbm, tile, mask, sems):
    width = tile.shape[1] // 2
    copies = []
    for place, column in enumerate((first, first + 1 - 2 * (first % 2))):
        source = pl.ds(pl.multiple_of(column * width, width), width)
        target = pl.ds(place * width, width)
        for i, (whole, part) in enumerate(((x_hbm, tile), (m_hbm, mask))):
            copies.append(
                pltpu.make_async_copy(whole.at[:, source], part.at[:, target], sems.at[2 * place + i])
            )
    return copies


def first_columns(place, blocks, hop, flip):
    block = lax.rem(place[0] // 2 + (blocks * HOPS - hop), blocks)
    side = place[0] % 2
    return 2 * block + (1 - side if flip else side)


def load_body(blocks, place, x_hbm, m_hbm, u_hbm, v_hbm, tile, mask, u, va, vb, sems):
    rows = va.shape[0]
    half = place[0] % 2
    copies = tile_copies(first_columns(place, blocks, 0, False), x_hbm, m_hbm, tile, mask, sems)
    copies.append(pltpu.make_async_copy(u_hbm, u, sems.at[4]))
    for order, (out, index) in enumerate(((va, half), (vb, 1 - half))):
        at = pl.ds(pl.multiple_of(index * rows, rows), rows)
        copies.append(pltpu.make_async_copy(v_hbm.at[at], out, sems.at[5 + order]))
    for copy in copies:
        copy.start()
    for copy in copies:
        copy.wait()


def open_body(steps, u, va, tile, mask, grad_u, va1):
    cell_half, locus_half = u[...].astype(HALF), va[...].astype(HALF)
    r = residue(tile, mask, 0, cell_half, locus_half)
    grad_u[...] = times(r, locus_half)
    va1[...] = va[...] + steps[1] * along(r, cell_half)


def turn_body(steps, u, grad_u, va1, vb, tile, mask, u1, va2, rest):
    width = vb.shape[0]
    cell_half, locus_half = u[...].astype(HALF), vb[...].astype(HALF)
    r = residue(tile, mask, 1, cell_half, locus_half)
    rest[:, width:] = r
    moved_u = u[...] + steps[0] * (grad_u[...] + times(r, locus_half))
    u1[...] = moved_u
    cell_half, locus_half = moved_u.astype(HALF), va1[...].astype(HALF)
    r = residue(tile, mask, 0, cell_half, locus_half)
    rest[:, :width] = r
    va2[...] = va1[...] + steps[1] * along(r, cell_half)


def close_body(steps, u, u1, rest, vb, tile, mask, vb2, vb1_half, r2b):
    width = vb.shape[0]
    vb1 = vb[...] + steps[1] * along(rest[:, width:], u[...].astype(HALF))
    cell_half, locus_half = u1[...].astype(HALF), vb1.astype(HALF)
    r = residue(tile, mask, 1, cell_half, locus_half)
    vb2[...] = vb1 + steps[1] * along(r, cell_half)
    vb1_half[...] = locus_half
    r2b[...] = r


def settle(steps, u1, rest, va1, vb1_half, r2b, u2):
    width = r2b.shape[1]
    grad_u = times(rest[:, :width], va1[...].astype(HALF)) + times(r2b[...], vb1_half[...])
    u2[...] = u1[...] + steps[0] * grad_u


def hold_body(steps, blocks, hop, place, u1, rest, va1, vb1_half, r2b, va2, vb2, x_hbm, m_hbm, u2, tile, mask, va, vb, sems):
    va[...] = va2[...]
    vb[...] = vb2[...]
    settle_body(steps, blocks, hop, hop >= HOPS // 2, place, u1, rest, va1, vb1_half, r2b, x_hbm, m_hbm, u2, tile, mask, sems)


def settle_body(steps, blocks, hop, flip, place, u1, rest, va1, vb1_half, r2b, x_hbm, m_hbm, u2, tile, mask, sems):
    copies = tile_copies(first_columns(place, blocks, hop, flip), x_hbm, m_hbm, tile, mask, sems)
    for copy in copies:
        copy.start()
    settle(steps, u1, rest, va1, vb1_half, r2b, u2)
    for copy in copies:
        copy.wait()


def call(body, args, spaces, outs, sems=0, flops=0):
    kinds = {"v": pltpu.VMEM, "h": pltpu.HBM, "s": pltpu.SMEM}
    pinned = [
        a if s == "s" else pltpu.with_memory_space_constraint(a, kinds[s])
        for a, s in zip(args, spaces)
    ]
    moved_bytes = sum(a.size * a.dtype.itemsize for a in args) if sems == 0 else 4 << 20
    return pl.pallas_call(
        body,
        out_shape=[jax.ShapeDtypeStruct(shape, dtype) for shape, dtype in outs],
        in_specs=[pl.BlockSpec(memory_space=kinds[s]) for s in spaces],
        out_specs=[pl.BlockSpec(memory_space=pltpu.VMEM) for _ in outs],
        scratch_shapes=[pltpu.SemaphoreType.DMA((sems,))] if sems else [],
        compiler_params=pltpu.CompilerParams(vmem_limit_bytes=8 << 20),
        cost_estimate=pl.CostEstimate(flops=flops, bytes_accessed=moved_bytes, transcendentals=0),
    )(*pinned)


def moved(block, blocks, groups, distance, flip=0, cores=(0, 1)):
    route = [
        (b * groups + g, (b + distance) % blocks * groups + (g ^ flip))
        for b in range(blocks)
        for g in range(groups)
        if g % 2 in cores
    ]
    return lax.ppermute(block, AXES, route)


def in_turns(parts, later, blocks, groups):
    first = [moved(part, blocks, groups, 1, cores=(0,)) for part in parts]
    second = [moved(part, blocks, groups, 1, cores=(1,)) for part in later]
    first = lax.optimization_barrier(first)
    return zip(first, second)


def average(part_a, part_b, pending, blocks, groups, distance):
    member = lax.axis_index("group")
    bits = [1 << i for i in range(1, groups.bit_length() - 1)]
    share = part_b + moved(part_a, blocks, groups, 0, 1)
    for bit in bits:
        rows = share.shape[0] // 2
        upper = (member & bit) != 0
        low, high = share[:rows], share[rows:]
        received = moved(jnp.where(upper, low, high), blocks, groups, 0, bit)
        received, *pending = lax.optimization_barrier((received, *pending))
        share = jnp.where(upper, high, low) + received
    share = share / groups
    for place, bit in enumerate(reversed(bits)):
        upper = (member & bit) != 0
        if place == 0:
            mine = moved(share, blocks, groups, distance)
            other = moved(share, blocks, groups, distance, bit)
        else:
            mine = share
            other = moved(share, blocks, groups, 0, bit)
        share = jnp.where(
            upper, jnp.concatenate([other, mine], 0), jnp.concatenate([mine, other], 0)
        )
    return share, moved(share, blocks, groups, 0, 1), pending


def solution(mesh):
    blocks, groups = mesh.shape["blk"], mesh.shape["group"]

    def on_device(expression, observed, cell_factors, locus_factors):
        position = lax.axis_index("blk")
        side = lax.axis_index("group") % 2
        cells, rank = cell_factors.shape
        rows = locus_factors.shape[0] // 2
        steps = (2.0 / (2 * rows + rank), 2.0 / (cells + rank))
        wide, tall = ((cells, rank), F32), ((rows, rank), F32)
        tiles = [((cells, 2 * rows), HALF), ((cells, 2 * rows), jnp.int32)]
        work = 2 * cells * rows * rank
        place = (2 * position + side).reshape(1).astype(jnp.int32)

        tile, mask, u, va, vb = call(
            functools.partial(load_body, blocks),
            (place, expression, observed, cell_factors, locus_factors),
            "shhhh",
            tiles + [wide, tall, tall],
            7,
        )
        for hop in range(HOPS):
            grad_u, va1 = call(
                functools.partial(open_body, steps), (u, va, tile, mask), "vvvv", [wide, tall], 0, 3 * work
            )
            if vb is None:
                va1, *pair_b = lax.optimization_barrier((va1, *pair_b))
                vb = jnp.where(side == 0, *pair_b)
            u1, va2, rest = call(
                functools.partial(turn_body, steps),
                (u, grad_u, va1, vb, tile, mask),
                "vvvvvv",
                [wide, tall, ((cells, 2 * rows), HALF)],
                0,
                4 * work,
            )
            vb2, vb1_half, r2b = call(
                functools.partial(close_body, steps),
                (u, u1, rest, vb, tile, mask),
                "vvvvvv",
                [tall, ((rows, rank), HALF), ((cells, rows), HALF)],
                0,
                3 * work,
            )
            turns = hop % (HOPS // 2) == 0
            if turns:
                u, tile, mask, *later = call(
                    functools.partial(hold_body, steps, blocks, hop + 1),
                    (place, u1, rest, va1, vb1_half, r2b, va2, vb2, expression, observed),
                    "svvvvvvvhh",
                    [wide] + tiles + [tall, tall],
                    4,
                    2 * work,
                )
            elif hop < HOPS - 1:
                u, tile, mask = call(
                    functools.partial(settle_body, steps, blocks, hop + 1, hop + 1 >= HOPS // 2),
                    (place, u1, rest, va1, vb1_half, r2b, expression, observed),
                    "svvvvvhh",
                    [wide] + tiles,
                    4,
                    2 * work,
                )
            else:
                (u,) = call(
                    functools.partial(settle, steps), (u1, rest, va1, vb1_half, r2b), "vvvvv", [wide], 0, 2 * work
                )
            if hop == HOPS // 2 - 1 or hop == HOPS - 1:
                distance = 1 if hop < HOPS - 1 else 1 - HOPS
                va, vb, (u, tile, mask) = average(va2, vb2, (u, tile, mask), blocks, groups, distance)
            elif turns:
                pair_a, pair_b = in_turns((va2, vb2), later, blocks, groups)
                va, vb = jnp.where(side == 0, *pair_a), None
            else:
                va, vb = (moved(part, blocks, groups, 1) for part in (va2, vb2))
        whole = jnp.where(side == 0, jnp.concatenate([va, vb], 0), jnp.concatenate([vb, va], 0))
        return u, whole

    split = P(AXES, None)
    return jax.shard_map(
        on_device,
        mesh=mesh,
        in_specs=(split, split, split, P("blk", None)),
        out_specs=(split, P("blk", None)),
        check_vma=False,
    )
```

```python
import functools

import jax
import jax.numpy as jnp
from jax import lax
from jax.experimental import pallas as pl
from jax.experimental.pallas import tpu as pltpu
from jax.sharding import PartitionSpec as P

HOPS = 6
AXES = ("blk", "group")
F32, HALF = jnp.float32, jnp.bfloat16


def across(a, b):
    return lax.dot_general(a, b, (((1,), (1,)), ((), ())), preferred_element_type=F32)


def along(a, b):
    return lax.dot_general(a, b, (((0,), (0,)), ((), ())), preferred_element_type=F32)


def times(a, b):
    return jnp.dot(a, b, preferred_element_type=F32)


def first_columns(place, blocks, hop, flip):
    block = lax.rem(place[0] // 2 + (blocks * HOPS - hop), blocks)
    side = place[0] % 2
    return 2 * block + (1 - side if flip else side)


def tile_copies(first, x_hbm, m_hbm, tile, mask, sems):
    width = tile.shape[1] // 2
    copies = []
    for order, column in enumerate((first, first + 1 - 2 * (first % 2))):
        source = pl.ds(pl.multiple_of(column * width, width), width)
        target = pl.ds(order * width, width)
        for i, (whole, part) in enumerate(((x_hbm, tile), (m_hbm, mask))):
            copies.append(
                pltpu.make_async_copy(whole.at[:, source], part.at[:, target], sems.at[2 * order + i])
            )
    return copies


def residue(tile, mask, cell_half, locus_half):
    return (mask[...] * (tile[...] - across(locus_half, cell_half))).astype(HALF)


def visit(steps, cells, loci, tile, mask, u1, v1_half, r2, v2):
    cell_half, locus_half = cells.astype(HALF), loci.astype(HALF)
    r = residue(tile, mask, cell_half, locus_half)
    cells = cells + steps[0] * along(r, locus_half)
    u1[...] = cells
    loci = loci + steps[1] * times(r, cell_half)
    cell_half, locus_half = cells.astype(HALF), loci.astype(HALF)
    v1_half[...] = locus_half
    r = residue(tile, mask, cell_half, locus_half)
    r2[...] = r
    loci = loci + steps[1] * times(r, cell_half)
    row = 0
    for out in v2:
        out[...] = loci[row : row + out.shape[0]]
        row += out.shape[0]


def start_body(steps, blocks, place, x_hbm, m_hbm, u_hbm, v_hbm, u1, v1_half, r2, v2, tile, mask, x, m, u, v, sems):
    rows = v.shape[0] // 2
    side = place[0] % 2
    copies = tile_copies(first_columns(place, blocks, 0, False), x_hbm, m_hbm, x, m, sems)
    inputs = [pltpu.make_async_copy(u_hbm, u, sems.at[4])]
    for order, index in enumerate((side, 1 - side)):
        source = pl.ds(pl.multiple_of(index * rows, rows), rows)
        target = pl.ds(order * rows, rows)
        inputs.append(pltpu.make_async_copy(v_hbm.at[source], v.at[target], sems.at[5 + order]))
    for copy in copies + inputs:
        copy.start()
    for copy in copies:
        copy.wait()
    tile[...] = x[...].astype(F32).T
    mask[...] = m[...].astype(F32).T
    for copy in inputs:
        copy.wait()
    visit(steps, u[...], v[...], tile, mask, u1, v1_half, r2, (v2,))


def visit_body(steps, parts, u, *refs):
    loci = jnp.concatenate([part[...] for part in refs[:parts]], 0)
    tile, mask, u1, v1_half, r2, *v2 = refs[parts:]
    visit(steps, u[...], loci, tile, mask, u1, v1_half, r2, v2)


def settle(steps, u1, v1_half, r2, u2):
    u2[...] = u1[...] + steps[0] * along(r2[...], v1_half[...])


def settle_body(steps, blocks, hop, flip, place, u1, v1_half, r2, x_hbm, m_hbm, u2, tile, mask, x, m, sems):
    copies = tile_copies(first_columns(place, blocks, hop, flip), x_hbm, m_hbm, x, m, sems)
    for copy in copies:
        copy.start()
    settle(steps, u1, v1_half, r2, u2)
    for copy in copies:
        copy.wait()
    tile[...] = x[...].astype(F32).T
    mask[...] = m[...].astype(F32).T


def call(body, args, spaces, outs, scratch=(), flops=0):
    kinds = {"v": pltpu.VMEM, "h": pltpu.HBM, "s": pltpu.SMEM}
    placed = [
        a if s == "s" else pltpu.with_memory_space_constraint(a, kinds[s])
        for a, s in zip(args, spaces)
    ]
    return pl.pallas_call(
        body,
        out_shape=[jax.ShapeDtypeStruct(shape, dtype) for shape, dtype in outs],
        in_specs=[pl.BlockSpec(memory_space=kinds[s]) for s in spaces],
        out_specs=[pl.BlockSpec(memory_space=pltpu.VMEM) for _ in outs],
        scratch_shapes=list(scratch),
        compiler_params=pltpu.CompilerParams(vmem_limit_bytes=12 << 20),
        cost_estimate=pl.CostEstimate(flops=flops, bytes_accessed=4 << 20, transcendentals=0),
    )(*placed)


def moved(block, blocks, groups, distance, flip=0):
    route = [
        (b * groups + g, (b + distance) % blocks * groups + (g ^ flip))
        for b in range(blocks)
        for g in range(groups)
    ]
    return lax.ppermute(block, AXES, route)


def average(part_a, part_b, pending, blocks, groups, distance):
    member = lax.axis_index("group")
    bits = [1 << i for i in range(1, groups.bit_length() - 1)]
    share = part_b + moved(part_a, blocks, groups, 0, 1)
    for bit in bits:
        rows = share.shape[0] // 2
        upper = (member & bit) != 0
        low, high = share[:rows], share[rows:]
        received = moved(jnp.where(upper, low, high), blocks, groups, 0, bit)
        received, *pending = lax.optimization_barrier((received, *pending))
        share = jnp.where(upper, high, low) + received
    share = share / groups
    for place, bit in enumerate(reversed(bits)):
        upper = (member & bit) != 0
        if place == 0:
            mine = moved(share, blocks, groups, distance)
            other = moved(share, blocks, groups, distance, bit)
        else:
            mine = share
            other = moved(share, blocks, groups, 0, bit)
        share = jnp.where(
            upper, jnp.concatenate([other, mine], 0), jnp.concatenate([mine, other], 0)
        )
    return share, moved(share, blocks, groups, 0, 1), pending


def solution(mesh):
    blocks, groups = mesh.shape["blk"], mesh.shape["group"]

    def on_device(expression, observed, cell_factors, locus_factors):
        position = lax.axis_index("blk")
        side = lax.axis_index("group") % 2
        cells, rank = cell_factors.shape
        loci = locus_factors.shape[0]
        steps = (2.0 / (loci + rank), 2.0 / (cells + rank))
        work = 2 * cells * loci * rank
        place = (2 * position + side).reshape(1).astype(jnp.int32)
        wide, tall, turned = ((cells, rank), F32), ((loci, rank), F32), ((loci, cells), F32)
        part = ((loci // 2, rank), F32)
        state = [wide, ((loci, rank), HALF), ((loci, cells), HALF)]
        fetched = [pltpu.VMEM((cells, loci), HALF), pltpu.VMEM((cells, loci), jnp.int32)]

        for hop in range(HOPS):
            averaged = (hop + 1) % (HOPS // 2) == 0
            if hop == 0:
                u1, v1_half, r2, v2 = call(
                    functools.partial(start_body, steps, blocks),
                    (place, expression, observed, cell_factors, locus_factors),
                    "shhhh",
                    state + [tall],
                    [
                        pltpu.VMEM(turned[0], F32),
                        pltpu.VMEM(turned[0], F32),
                        *fetched,
                        pltpu.VMEM(wide[0], F32),
                        pltpu.VMEM(tall[0], F32),
                        pltpu.SemaphoreType.DMA((7,)),
                    ],
                    5 * work,
                )
                v2 = [v2]
            else:
                u1, v1_half, r2, *v2 = call(
                    functools.partial(visit_body, steps, len(parts)),
                    (u, *parts, tile, mask),
                    "v" * (3 + len(parts)),
                    state + ([part, part] if averaged else [tall]),
                    (),
                    5 * work,
                )
            if hop < HOPS - 1:
                u, tile, mask = call(
                    functools.partial(settle_body, steps, blocks, hop + 1, hop + 1 >= HOPS // 2),
                    (place, u1, v1_half, r2, expression, observed),
                    "svvvhh",
                    [wide, turned, turned],
                    fetched + [pltpu.SemaphoreType.DMA((4,))],
                    work,
                )
                pending = (u, tile, mask)
            else:
                pending = call(functools.partial(settle, steps), (u1, v1_half, r2), "vvv", [wide], (), work)
            if averaged:
                distance = 1 if hop < HOPS - 1 else 1 - HOPS
                *parts, pending = average(*v2, pending, blocks, groups, distance)
                u, *rest = pending
                if rest:
                    tile, mask = rest
            else:
                parts = [moved(v2[0], blocks, groups, 1)]
        low, high = parts
        return u, jnp.where(side == 0, jnp.concatenate([low, high], 0), jnp.concatenate([high, low], 0))

    split = P(AXES, None)
    return jax.shard_map(
        on_device,
        mesh=mesh,
        in_specs=(split, split, split, P("blk", None)),
        out_specs=(split, P("blk", None)),
        check_vma=False,
    )
```

```python
import functools

import jax
import jax.numpy as jnp
from jax import lax
from jax.experimental import pallas as pl
from jax.experimental.pallas import tpu as pltpu
from jax.sharding import PartitionSpec as P

HOPS = 6
AXES = ("blk", "group")
F32, HALF = jnp.float32, jnp.bfloat16


def across(a, b):
    return lax.dot_general(a, b, (((1,), (1,)), ((), ())), preferred_element_type=F32)


def along(a, b):
    return lax.dot_general(a, b, (((0,), (0,)), ((), ())), preferred_element_type=F32)


def times(a, b):
    return jnp.dot(a, b, preferred_element_type=F32)


def first_columns(place, blocks, hop, flip):
    block = lax.rem(place[0] // 2 + (blocks * HOPS - hop), blocks)
    side = place[0] % 2
    return 2 * block + (1 - side if flip else side)


def tile_copies(first, x_hbm, m_hbm, tile, mask, sems):
    width = tile.shape[1] // 2
    copies = []
    for order, column in enumerate((first, first + 1 - 2 * (first % 2))):
        source = pl.ds(pl.multiple_of(column * width, width), width)
        target = pl.ds(order * width, width)
        for i, (whole, part) in enumerate(((x_hbm, tile), (m_hbm, mask))):
            copies.append(
                pltpu.make_async_copy(whole.at[:, source], part.at[:, target], sems.at[2 * order + i])
            )
    return copies


def residue(tile, mask, cell_half, locus_half):
    return (mask[...] * (tile[...] - across(locus_half, cell_half))).astype(HALF)


def visit(steps, cells, loci, tile, mask, u1, v1_half, r2, v2):
    cell_half, locus_half = cells.astype(HALF), loci.astype(HALF)
    r = residue(tile, mask, cell_half, locus_half)
    cells = cells + steps[0] * along(r, locus_half)
    u1[...] = cells
    loci = loci + steps[1] * times(r, cell_half)
    cell_half, locus_half = cells.astype(HALF), loci.astype(HALF)
    v1_half[...] = locus_half
    r = residue(tile, mask, cell_half, locus_half)
    r2[...] = r
    loci = loci + steps[1] * times(r, cell_half)
    row = 0
    for out in v2:
        out[...] = loci[row : row + out.shape[0]]
        row += out.shape[0]


def parity(place):
    return place[0] // 2 % 2


def start_body(steps, blocks, turn, place, x_hbm, m_hbm, u_hbm, v_hbm, u1, v1_half, r2, v2, tile, mask, x, m, u, v, sems):
    @pl.when(parity(place) == turn)
    def _():
        rows = v.shape[0] // 2
        side = place[0] % 2
        copies = tile_copies(first_columns(place, blocks, 0, False), x_hbm, m_hbm, x, m, sems)
        inputs = [pltpu.make_async_copy(u_hbm, u, sems.at[4])]
        for order, index in enumerate((side, 1 - side)):
            source = pl.ds(pl.multiple_of(index * rows, rows), rows)
            target = pl.ds(order * rows, rows)
            inputs.append(pltpu.make_async_copy(v_hbm.at[source], v.at[target], sems.at[5 + order]))
        for copy in copies + inputs:
            copy.start()
        for copy in copies:
            copy.wait()
        tile[...] = x[...].astype(F32).T
        mask[...] = m[...].astype(F32).T
        for copy in inputs:
            copy.wait()
        visit(steps, u[...], v[...], tile, mask, u1, v1_half, r2, (v2,))


def turn_body(steps, turn, parts, place, u, *refs):
    @pl.when(parity(place) == turn)
    def _():
        loci = jnp.concatenate([part[...] for part in refs[:parts]], 0)
        tile, mask, u1, v1_half, r2, *v2 = refs[parts:]
        visit(steps, u[...], loci, tile, mask, u1, v1_half, r2, v2)


def visit_body(steps, place, u, even, odd, tile, mask, u1, v1_half, r2, *v2):
    @pl.when(parity(place) == 0)
    def _():
        visit(steps, u[...], even[...], tile, mask, u1, v1_half, r2, v2)

    @pl.when(parity(place) == 1)
    def _():
        visit(steps, u[...], odd[...], tile, mask, u1, v1_half, r2, v2)


def settle(steps, place, states, u2):
    for turn, (u1, v1_half, r2) in enumerate(states):

        @pl.when(parity(place) == turn)
        def _():
            u2[...] = u1[...] + steps[0] * along(r2[...], v1_half[...])


def settle_body(steps, blocks, hop, flip, count, place, *refs):
    states, (x_hbm, m_hbm, u2, tile, mask, x, m, sems) = refs[: 3 * count], refs[3 * count :]
    copies = tile_copies(first_columns(place, blocks, hop, flip), x_hbm, m_hbm, x, m, sems)
    for copy in copies:
        copy.start()
    if count == 1:
        u1, v1_half, r2 = states
        u2[...] = u1[...] + steps[0] * along(r2[...], v1_half[...])
    else:
        settle(steps, place, (states[:3], states[3:]), u2)
    for copy in copies:
        copy.wait()
    tile[...] = x[...].astype(F32).T
    mask[...] = m[...].astype(F32).T


def finish_body(steps, u1, v1_half, r2, u2):
    u2[...] = u1[...] + steps[0] * along(r2[...], v1_half[...])


def call(body, args, spaces, outs, scratch=(), flops=0):
    kinds = {"v": pltpu.VMEM, "h": pltpu.HBM, "s": pltpu.SMEM}
    placed = [
        a if s == "s" else pltpu.with_memory_space_constraint(a, kinds[s])
        for a, s in zip(args, spaces)
    ]
    return pl.pallas_call(
        body,
        out_shape=[jax.ShapeDtypeStruct(shape, dtype) for shape, dtype in outs],
        in_specs=[pl.BlockSpec(memory_space=kinds[s]) for s in spaces],
        out_specs=[pl.BlockSpec(memory_space=pltpu.VMEM) for _ in outs],
        scratch_shapes=list(scratch),
        compiler_params=pltpu.CompilerParams(vmem_limit_bytes=12 << 20),
        cost_estimate=pl.CostEstimate(flops=flops, bytes_accessed=4 << 20, transcendentals=0),
    )(*placed)


def moved(block, blocks, groups, distance, flip=0, senders=(0, 1)):
    route = [
        (b * groups + g, (b + distance) % blocks * groups + (g ^ flip))
        for b in range(blocks)
        for g in range(groups)
        if b % 2 in senders
    ]
    return lax.ppermute(block, AXES, route)


def average(part_a, part_b, pending, blocks, groups, distance):
    member = lax.axis_index("group")
    bits = [1 << i for i in range(1, groups.bit_length() - 1)]
    share = part_b + moved(part_a, blocks, groups, 0, 1)
    for bit in bits:
        rows = share.shape[0] // 2
        upper = (member & bit) != 0
        low, high = share[:rows], share[rows:]
        received = moved(jnp.where(upper, low, high), blocks, groups, 0, bit)
        received, *pending = lax.optimization_barrier((received, *pending))
        share = jnp.where(upper, high, low) + received
    share = share / groups
    for place, bit in enumerate(reversed(bits)):
        upper = (member & bit) != 0
        if place == 0:
            mine = moved(share, blocks, groups, distance)
            other = moved(share, blocks, groups, distance, bit)
        else:
            mine = share
            other = moved(share, blocks, groups, 0, bit)
        share = jnp.where(
            upper, jnp.concatenate([other, mine], 0), jnp.concatenate([mine, other], 0)
        )
    return share, moved(share, blocks, groups, 0, 1), pending


def solution(mesh):
    blocks, groups = mesh.shape["blk"], mesh.shape["group"]

    def on_device(expression, observed, cell_factors, locus_factors):
        position = lax.axis_index("blk")
        side = lax.axis_index("group") % 2
        cells, rank = cell_factors.shape
        loci = locus_factors.shape[0]
        steps = (2.0 / (loci + rank), 2.0 / (cells + rank))
        work = 2 * cells * loci * rank
        place = (2 * position + side).reshape(1).astype(jnp.int32)
        wide, tall, turned = ((cells, rank), F32), ((loci, rank), F32), ((loci, cells), F32)
        part = ((loci // 2, rank), F32)
        state = [wide, ((loci, rank), HALF), ((loci, cells), HALF)]
        fetched = [pltpu.VMEM((cells, loci), HALF), pltpu.VMEM((cells, loci), jnp.int32)]

        def turns(u, parts, tile, mask):
            states, gots = [], []
            for turn in (1, 0):
                if u is None:
                    *state_of, v2 = call(
                        functools.partial(start_body, steps, blocks, turn),
                        (place, expression, observed, cell_factors, locus_factors),
                        "shhhh",
                        state + [tall],
                        [
                            pltpu.VMEM(turned[0], F32),
                            pltpu.VMEM(turned[0], F32),
                            *fetched,
                            pltpu.VMEM(wide[0], F32),
                            pltpu.VMEM(tall[0], F32),
                            pltpu.SemaphoreType.DMA((7,)),
                        ],
                        5 * work,
                    )
                else:
                    mine = parts[turn]
                    *state_of, v2 = call(
                        functools.partial(turn_body, steps, turn, len(mine)),
                        (place, u, *mine, tile, mask),
                        "s" + "v" * (3 + len(mine)),
                        state + [tall],
                        (),
                        5 * work,
                    )
                states.append(state_of)
                gots.append(moved(v2, blocks, groups, 1, senders=(turn,)))
            return states[1] + states[0], gots

        def settled(hop, states):
            return call(
                functools.partial(settle_body, steps, blocks, hop, hop >= HOPS // 2, len(states) // 3),
                (place, *states, expression, observed),
                "s" + "v" * len(states) + "hh",
                [wide, turned, turned],
                fetched + [pltpu.SemaphoreType.DMA((4,))],
                work,
            )

        u = tile = mask = parts = None
        for hop in range(HOPS):
            if (hop + 1) % (HOPS // 2):
                states, (even, odd) = turns(u, parts, tile, mask)
                u, tile, mask = settled(hop + 1, states)
                parts = [even], [odd]
                continue
            u1, v1_half, r2, *v2 = call(
                functools.partial(visit_body, steps),
                (place, u, even, odd, tile, mask),
                "svvvvv",
                state + [part, part],
                (),
                5 * work,
            )
            if hop < HOPS - 1:
                pending = settled(hop + 1, (u1, v1_half, r2))
            else:
                pending = call(functools.partial(finish_body, steps), (u1, v1_half, r2), "vvv", [wide], (), work)
            distance = 1 if hop < HOPS - 1 else 1 - HOPS
            *parts, pending = average(*v2, pending, blocks, groups, distance)
            if hop < HOPS - 1:
                (u, tile, mask), parts = pending, (parts, parts)
        (u,), (low, high) = pending, parts
        return u, jnp.where(side == 0, jnp.concatenate([low, high], 0), jnp.concatenate([high, low], 0))

    split = P(AXES, None)
    return jax.shard_map(
        on_device,
        mesh=mesh,
        in_specs=(split, split, split, P("blk", None)),
        out_specs=(split, P("blk", None)),
        check_vma=False,
    )
```

```python
import functools

import jax
import jax.numpy as jnp
from jax import lax
from jax.experimental import pallas as pl
from jax.experimental.pallas import tpu as pltpu
from jax.sharding import PartitionSpec as P

HOPS = 6
AXES = ("blk", "group")
F32, HALF = jnp.float32, jnp.bfloat16


def across(a, b):
    return lax.dot_general(a, b, (((1,), (1,)), ((), ())), preferred_element_type=F32)


def along(a, b):
    return lax.dot_general(a, b, (((0,), (0,)), ((), ())), preferred_element_type=F32)


def times(a, b):
    return jnp.dot(a, b, preferred_element_type=F32)


def first_columns(place, blocks, hop, flip):
    block = lax.rem(place[0] // 2 + (blocks * HOPS - hop), blocks)
    side = place[0] % 2
    return 2 * block + (1 - side if flip else side)


def tile_copies(first, x_hbm, m_hbm, tile, mask, sems):
    width = tile.shape[1] // 2
    copies = []
    for order, column in enumerate((first, first + 1 - 2 * (first % 2))):
        source = pl.ds(pl.multiple_of(column * width, width), width)
        target = pl.ds(order * width, width)
        for i, (whole, part) in enumerate(((x_hbm, tile), (m_hbm, mask))):
            copies.append(
                pltpu.make_async_copy(whole.at[:, source], part.at[:, target], sems.at[2 * order + i])
            )
    return copies


def residue(tile, mask, predicted):
    return (mask * (tile - predicted)).astype(HALF)


def visit(steps, cells, loci, tile, mask, u1, v1_half, r2, v2, fetch=lambda: None):
    cell_half, locus_half = cells.astype(HALF), loci.astype(HALF)
    predicted = across(locus_half, cell_half)
    fetch()
    r = residue(tile[...], mask[...], predicted)
    cells = cells + steps[0] * along(r, locus_half)
    u1[...] = cells
    loci = loci + steps[1] * times(r, cell_half)
    cell_half, locus_half = cells.astype(HALF), loci.astype(HALF)
    v1_half[...] = locus_half
    rows = v2[0].shape[0]
    r = residue(tile[:rows], mask[:rows], across(locus_half[:rows], cell_half))
    r2[...] = r
    v2[0][...] = loci[:rows] + steps[1] * times(r, cell_half)
    for v1 in v2[1:]:
        v1[...] = loci[rows:]


def rest_body(steps, u1, v1_half, v1, tile, mask, r2, v2):
    rows = v1.shape[0]
    cell_half = u1[...].astype(HALF)
    r = residue(tile[rows:], mask[rows:], across(v1_half[rows:], cell_half))
    r2[...] = r
    v2[...] = v1[...] + steps[1] * times(r, cell_half)


def start_body(steps, blocks, place, x_hbm, m_hbm, u_hbm, v_hbm, u1, v1_half, r2, v2, tile, mask, x, m, u, v, sems):
    rows = v.shape[0] // 2
    side = place[0] % 2
    copies = tile_copies(first_columns(place, blocks, 0, False), x_hbm, m_hbm, x, m, sems)
    inputs = [pltpu.make_async_copy(u_hbm, u, sems.at[4])]
    for order, index in enumerate((side, 1 - side)):
        source = pl.ds(pl.multiple_of(index * rows, rows), rows)
        target = pl.ds(order * rows, rows)
        inputs.append(pltpu.make_async_copy(v_hbm.at[source], v.at[target], sems.at[5 + order]))
    for copy in inputs + copies:
        copy.start()

    def fetch():
        for copy in copies:
            copy.wait()
        tile[...] = x[...].astype(F32).T
        mask[...] = m[...].astype(F32).T

    for copy in inputs:
        copy.wait()
    visit(steps, u[...], v[...], tile, mask, u1, v1_half, r2, (v2,), fetch)


def visit_body(steps, parts, u, *refs):
    loci = jnp.concatenate([part[...] for part in refs[:parts]], 0)
    tile, mask, u1, v1_half, r2, *v2 = refs[parts:]
    visit(steps, u[...], loci, tile, mask, u1, v1_half, r2, v2)


def settle(steps, u1, v1_half, residues, u2):
    r2 = residues[0][...] if len(residues) == 1 else jnp.concatenate([r[...] for r in residues], 0)
    u2[...] = u1[...] + steps[0] * along(r2, v1_half[...])


def settle_body(steps, blocks, hop, flip, place, u1, v1_half, *refs):
    *residues, x_hbm, m_hbm, u2, tile, mask, x, m, sems = refs
    copies = tile_copies(first_columns(place, blocks, hop, flip), x_hbm, m_hbm, x, m, sems)
    for copy in copies:
        copy.start()
    settle(steps, u1, v1_half, residues, u2)
    for copy in copies:
        copy.wait()
    tile[...] = x[...].astype(F32).T
    mask[...] = m[...].astype(F32).T


def finish_body(steps, u1, v1_half, *refs):
    *residues, u2 = refs
    settle(steps, u1, v1_half, residues, u2)


def store_body(place, first, second, out, sems):
    rows = first.shape[0]
    side = place[0] % 2
    copies = []
    for order, (half, index) in enumerate(((first, side), (second, 1 - side))):
        target = pl.ds(pl.multiple_of(index * rows, rows), rows)
        copies.append(pltpu.make_async_copy(half, out.at[target], sems.at[order]))
    for copy in copies:
        copy.start()
    for copy in copies:
        copy.wait()


def call(body, args, spaces, outs, scratch=(), flops=0, made=pltpu.VMEM):
    kinds = {"v": pltpu.VMEM, "h": pltpu.HBM, "s": pltpu.SMEM}
    placed = [
        a if s == "s" else pltpu.with_memory_space_constraint(a, kinds[s])
        for a, s in zip(args, spaces)
    ]
    return pl.pallas_call(
        body,
        out_shape=[jax.ShapeDtypeStruct(shape, dtype) for shape, dtype in outs],
        in_specs=[pl.BlockSpec(memory_space=kinds[s]) for s in spaces],
        out_specs=[pl.BlockSpec(memory_space=made) for _ in outs],
        scratch_shapes=list(scratch),
        compiler_params=pltpu.CompilerParams(vmem_limit_bytes=12 << 20),
        cost_estimate=pl.CostEstimate(flops=flops, bytes_accessed=4 << 20, transcendentals=0),
    )(*placed)


def moved(block, blocks, groups, distance, flip=0):
    route = [
        (b * groups + g, (b + distance) % blocks * groups + (g ^ flip))
        for b in range(blocks)
        for g in range(groups)
    ]
    return lax.ppermute(block, AXES, route)


def average(part_a, part_b, pending, blocks, groups, distance):
    member = lax.axis_index("group")
    bits = [1 << i for i in range(1, groups.bit_length() - 1)]
    share = part_b + moved(part_a, blocks, groups, 0, 1)
    for bit in bits:
        rows = share.shape[0] // 2
        upper = (member & bit) != 0
        low, high = share[:rows], share[rows:]
        received = moved(jnp.where(upper, low, high), blocks, groups, 0, bit)
        received, *pending = lax.optimization_barrier((received, *pending))
        share = jnp.where(upper, high, low) + received
    share = share / groups
    for place, bit in enumerate(reversed(bits)):
        upper = (member & bit) != 0
        if place == 0:
            mine = moved(share, blocks, groups, distance)
            other = moved(share, blocks, groups, distance, bit)
        else:
            mine = share
            other = moved(share, blocks, groups, 0, bit)
        share = jnp.where(
            upper, jnp.concatenate([other, mine], 0), jnp.concatenate([mine, other], 0)
        )
    return share, moved(share, blocks, groups, 0, 1), pending


def solution(mesh):
    blocks, groups = mesh.shape["blk"], mesh.shape["group"]

    def on_device(expression, observed, cell_factors, locus_factors):
        position = lax.axis_index("blk")
        side = lax.axis_index("group") % 2
        cells, rank = cell_factors.shape
        loci = locus_factors.shape[0]
        steps = (2.0 / (loci + rank), 2.0 / (cells + rank))
        work = 2 * cells * loci * rank
        place = (2 * position + side).reshape(1).astype(jnp.int32)
        wide, tall, turned = ((cells, rank), F32), ((loci, rank), F32), ((loci, cells), F32)
        part = ((loci // 2, rank), F32)
        state = [wide, ((loci, rank), HALF), ((loci, cells), HALF)]
        fetched = [pltpu.VMEM((cells, loci), HALF), pltpu.VMEM((cells, loci), jnp.int32)]

        for hop in range(HOPS):
            averaged = (hop + 1) % (HOPS // 2) == 0
            if hop == 0:
                u1, v1_half, r2, v2 = call(
                    functools.partial(start_body, steps, blocks),
                    (place, expression, observed, cell_factors, locus_factors),
                    "shhhh",
                    state + [tall],
                    [
                        pltpu.VMEM(turned[0], F32),
                        pltpu.VMEM(turned[0], F32),
                        *fetched,
                        pltpu.VMEM(wide[0], F32),
                        pltpu.VMEM(tall[0], F32),
                        pltpu.SemaphoreType.DMA((7,)),
                    ],
                    5 * work,
                )
                v2 = [v2]
            else:
                if averaged:
                    state = [wide, ((loci, rank), HALF), ((loci // 2, cells), HALF)]
                else:
                    state = [wide, ((loci, rank), HALF), ((loci, cells), HALF)]
                u1, v1_half, r2, *v2 = call(
                    functools.partial(visit_body, steps, len(parts)),
                    (u, *parts, tile, mask),
                    "v" * (3 + len(parts)),
                    state + ([part, part] if averaged else [tall]),
                    (),
                    5 * work,
                )
            residues = [r2]
            if averaged:
                va2, vb1 = v2
                r2b, vb2 = call(
                    functools.partial(rest_body, steps),
                    (u1, v1_half, vb1, tile, mask),
                    "vvvvv",
                    [((loci // 2, cells), HALF), part],
                    (),
                    work,
                )
                v2 = [va2, vb2]
                residues = [r2, r2b]
            if hop < HOPS - 1:
                u, tile, mask = call(
                    functools.partial(settle_body, steps, blocks, hop + 1, hop + 1 >= HOPS // 2),
                    (place, u1, v1_half, *residues, expression, observed),
                    "svv" + "v" * len(residues) + "hh",
                    [wide, turned, turned],
                    fetched + [pltpu.SemaphoreType.DMA((4,))],
                    work,
                )
                pending = (u, tile, mask)
            else:
                pending = call(functools.partial(finish_body, steps), (u1, v1_half, *residues), "vvvv", [wide], (), work)
            if averaged:
                distance = 1 if hop < HOPS - 1 else 1 - HOPS
                *parts, pending = average(*v2, pending, blocks, groups, distance)
                u, *rest = pending
                if rest:
                    tile, mask = rest
            else:
                parts = [moved(v2[0], blocks, groups, 1)]
        (whole,) = call(
            store_body, (place, *parts), "svv", [tall], [pltpu.SemaphoreType.DMA((2,))], made=pltpu.HBM
        )
        return u, whole

    split = P(AXES, None)
    return jax.shard_map(
        on_device,
        mesh=mesh,
        in_specs=(split, split, split, P("blk", None)),
        out_specs=(split, P("blk", None)),
        check_vma=False,
    )
```

```python
import functools

import jax
import jax.numpy as jnp
from jax import lax
from jax.experimental import pallas as pl
from jax.experimental.pallas import tpu as pltpu
from jax.sharding import PartitionSpec as P

HOPS = 6
AXES = ("blk", "group")
F32, HALF = jnp.float32, jnp.bfloat16


def across(a, b):
    return lax.dot_general(a, b, (((1,), (1,)), ((), ())), preferred_element_type=F32)


def along(a, b):
    return lax.dot_general(a, b, (((0,), (0,)), ((), ())), preferred_element_type=F32)


def times(a, b):
    return jnp.dot(a, b, preferred_element_type=F32)


def first_columns(place, blocks, hop, flip):
    block = lax.rem(place[0] // 2 + (blocks * HOPS - hop), blocks)
    side = place[0] % 2
    return 2 * block + (1 - side if flip else side)


def tile_copies(first, x_hbm, m_hbm, tile, mask, sems):
    width = tile.shape[1] // 2
    copies = []
    for order, column in enumerate((first, first + 1 - 2 * (first % 2))):
        source = pl.ds(pl.multiple_of(column * width, width), width)
        target = pl.ds(order * width, width)
        for i, (whole, part) in enumerate(((x_hbm, tile), (m_hbm, mask))):
            copies.append(
                pltpu.make_async_copy(whole.at[:, source], part.at[:, target], sems.at[2 * order + i])
            )
    return copies


def residue(tile, mask, predicted):
    return (mask * (tile - predicted)).astype(HALF)


def visit(steps, cells, loci, tile, mask, u1, v1_half, r2, v2, fetch=lambda: None):
    cell_half, locus_half = cells.astype(HALF), loci.astype(HALF)
    predicted = across(locus_half, cell_half)
    fetch()
    r = residue(tile[...], mask[...], predicted)
    loci = loci + steps[1] * times(r, cell_half)
    grad_cells = along(r, locus_half)
    locus_half = loci.astype(HALF)
    v1_half[...] = locus_half
    cells = cells + steps[0] * grad_cells
    u1[...] = cells
    cell_half = cells.astype(HALF)
    rows = v2[0].shape[0]
    r = residue(tile[:rows], mask[:rows], across(locus_half[:rows], cell_half))
    r2[...] = r
    v2[0][...] = loci[:rows] + steps[1] * times(r, cell_half)
    for v1 in v2[1:]:
        v1[...] = loci[rows:]


def rest_body(steps, u1, v1_half, v1, tile, mask, r2, v2):
    rows = v1.shape[0]
    cell_half = u1[...].astype(HALF)
    r = residue(tile[rows:], mask[rows:], across(v1_half[rows:], cell_half))
    r2[...] = r
    v2[...] = v1[...] + steps[1] * times(r, cell_half)


def start_body(steps, blocks, place, x_hbm, m_hbm, u_hbm, v_hbm, u1, v1_half, r2, v2, tile, mask, x, m, u, v, sems):
    rows = v.shape[0] // 2
    side = place[0] % 2
    copies = tile_copies(first_columns(place, blocks, 0, False), x_hbm, m_hbm, x, m, sems)
    inputs = [pltpu.make_async_copy(u_hbm, u, sems.at[4])]
    for order, index in enumerate((side, 1 - side)):
        source = pl.ds(pl.multiple_of(index * rows, rows), rows)
        target = pl.ds(order * rows, rows)
        inputs.append(pltpu.make_async_copy(v_hbm.at[source], v.at[target], sems.at[5 + order]))
    for copy in inputs + copies:
        copy.start()

    def fetch():
        for copy in copies:
            copy.wait()
        tile[...] = x[...].astype(F32).T
        mask[...] = m[...].astype(F32).T

    for copy in inputs:
        copy.wait()
    visit(steps, u[...], v[...], tile, mask, u1, v1_half, r2, (v2,), fetch)


def visit_body(steps, parts, u, *refs):
    loci = jnp.concatenate([part[...] for part in refs[:parts]], 0)
    tile, mask, u1, v1_half, r2, *v2 = refs[parts:]
    visit(steps, u[...], loci, tile, mask, u1, v1_half, r2, v2)


def settle(steps, u1, v1_half, residues, u2):
    r2 = residues[0][...] if len(residues) == 1 else jnp.concatenate([r[...] for r in residues], 0)
    u2[...] = u1[...] + steps[0] * along(r2, v1_half[...])


def settle_body(steps, blocks, hop, flip, place, u1, v1_half, *refs):
    *residues, x_hbm, m_hbm, u2, tile, mask, x, m, sems = refs
    copies = tile_copies(first_columns(place, blocks, hop, flip), x_hbm, m_hbm, x, m, sems)
    for copy in copies:
        copy.start()
    settle(steps, u1, v1_half, residues, u2)
    for copy in copies:
        copy.wait()
    tile[...] = x[...].astype(F32).T
    mask[...] = m[...].astype(F32).T


def finish_body(steps, u1, v1_half, *refs):
    *residues, u2 = refs
    settle(steps, u1, v1_half, residues, u2)


def store_body(place, first, second, out, sems):
    rows = first.shape[0]
    side = place[0] % 2
    copies = []
    for order, (half, index) in enumerate(((first, side), (second, 1 - side))):
        target = pl.ds(pl.multiple_of(index * rows, rows), rows)
        copies.append(pltpu.make_async_copy(half, out.at[target], sems.at[order]))
    for copy in copies:
        copy.start()
    for copy in copies:
        copy.wait()


def call(body, args, spaces, outs, scratch=(), flops=0, made=pltpu.VMEM):
    kinds = {"v": pltpu.VMEM, "h": pltpu.HBM, "s": pltpu.SMEM}
    placed = [
        a if s == "s" else pltpu.with_memory_space_constraint(a, kinds[s])
        for a, s in zip(args, spaces)
    ]
    return pl.pallas_call(
        body,
        out_shape=[jax.ShapeDtypeStruct(shape, dtype) for shape, dtype in outs],
        in_specs=[pl.BlockSpec(memory_space=kinds[s]) for s in spaces],
        out_specs=[pl.BlockSpec(memory_space=made) for _ in outs],
        scratch_shapes=list(scratch),
        compiler_params=pltpu.CompilerParams(vmem_limit_bytes=12 << 20),
        cost_estimate=pl.CostEstimate(flops=flops, bytes_accessed=4 << 20, transcendentals=0),
    )(*placed)


def moved(block, blocks, groups, distance, flip=0):
    route = [
        (b * groups + g, (b + distance) % blocks * groups + (g ^ flip))
        for b in range(blocks)
        for g in range(groups)
    ]
    return lax.ppermute(block, AXES, route)


def average(part_a, part_b, pending, blocks, groups, distance):
    member = lax.axis_index("group")
    bits = [1 << i for i in range(1, groups.bit_length() - 1)]
    share = part_b + moved(part_a, blocks, groups, 0, 1)
    for bit in bits:
        rows = share.shape[0] // 2
        upper = (member & bit) != 0
        low, high = share[:rows], share[rows:]
        received = moved(jnp.where(upper, low, high), blocks, groups, 0, bit)
        received, *pending = lax.optimization_barrier((received, *pending))
        share = jnp.where(upper, high, low) + received
    share = share / groups
    for place, bit in enumerate(reversed(bits)):
        upper = (member & bit) != 0
        if place == 0:
            mine = moved(share, blocks, groups, distance)
            other = moved(share, blocks, groups, distance, bit)
        else:
            mine = share
            other = moved(share, blocks, groups, 0, bit)
        share = jnp.where(
            upper, jnp.concatenate([other, mine], 0), jnp.concatenate([mine, other], 0)
        )
    return share, moved(share, blocks, groups, 0, 1), pending


def solution(mesh):
    blocks, groups = mesh.shape["blk"], mesh.shape["group"]

    def on_device(expression, observed, cell_factors, locus_factors):
        position = lax.axis_index("blk")
        side = lax.axis_index("group") % 2
        cells, rank = cell_factors.shape
        loci = locus_factors.shape[0]
        steps = (2.0 / (loci + rank), 2.0 / (cells + rank))
        work = 2 * cells * loci * rank
        place = (2 * position + side).reshape(1).astype(jnp.int32)
        wide, tall, turned = ((cells, rank), F32), ((loci, rank), F32), ((loci, cells), F32)
        part = ((loci // 2, rank), F32)
        state = [wide, ((loci, rank), HALF), ((loci, cells), HALF)]
        fetched = [pltpu.VMEM((cells, loci), HALF), pltpu.VMEM((cells, loci), jnp.int32)]

        for hop in range(HOPS):
            averaged = (hop + 1) % (HOPS // 2) == 0
            if hop == 0:
                u1, v1_half, r2, v2 = call(
                    functools.partial(start_body, steps, blocks),
                    (place, expression, observed, cell_factors, locus_factors),
                    "shhhh",
                    state + [tall],
                    [
                        pltpu.VMEM(turned[0], F32),
                        pltpu.VMEM(turned[0], F32),
                        *fetched,
                        pltpu.VMEM(wide[0], F32),
                        pltpu.VMEM(tall[0], F32),
                        pltpu.SemaphoreType.DMA((7,)),
                    ],
                    5 * work,
                )
                v2 = [v2]
            else:
                if averaged:
                    state = [wide, ((loci, rank), HALF), ((loci // 2, cells), HALF)]
                else:
                    state = [wide, ((loci, rank), HALF), ((loci, cells), HALF)]
                u1, v1_half, r2, *v2 = call(
                    functools.partial(visit_body, steps, len(parts)),
                    (u, *parts, tile, mask),
                    "v" * (3 + len(parts)),
                    state + ([part, part] if averaged else [tall]),
                    (),
                    5 * work,
                )
            residues = [r2]
            if averaged:
                va2, vb1 = v2
                r2b, vb2 = call(
                    functools.partial(rest_body, steps),
                    (u1, v1_half, vb1, tile, mask),
                    "vvvvv",
                    [((loci // 2, cells), HALF), part],
                    (),
                    work,
                )
                v2 = [va2, vb2]
                residues = [r2, r2b]
            if hop < HOPS - 1:
                u, tile, mask = call(
                    functools.partial(settle_body, steps, blocks, hop + 1, hop + 1 >= HOPS // 2),
                    (place, u1, v1_half, *residues, expression, observed),
                    "svv" + "v" * len(residues) + "hh",
                    [wide, turned, turned],
                    fetched + [pltpu.SemaphoreType.DMA((4,))],
                    work,
                )
                pending = (u, tile, mask)
            else:
                pending = call(functools.partial(finish_body, steps), (u1, v1_half, *residues), "vvvv", [wide], (), work)
            if averaged:
                distance = 1 if hop < HOPS - 1 else 1 - HOPS
                *parts, pending = average(*v2, pending, blocks, groups, distance)
                u, *rest = pending
                if rest:
                    tile, mask = rest
            else:
                parts = [moved(v2[0], blocks, groups, 1)]
        (whole,) = call(
            store_body, (place, *parts), "svv", [tall], [pltpu.SemaphoreType.DMA((2,))], made=pltpu.HBM
        )
        return u, whole

    split = P(AXES, None)
    return jax.shard_map(
        on_device,
        mesh=mesh,
        in_specs=(split, split, split, P("blk", None)),
        out_specs=(split, P("blk", None)),
        check_vma=False,
    )
```

```python
import functools

import jax
import jax.numpy as jnp
from jax import lax
from jax.experimental import pallas as pl
from jax.experimental.pallas import tpu as pltpu
from jax.sharding import PartitionSpec as P

HOPS = 6
AXES = ("blk", "group")
F32, HALF = jnp.float32, jnp.bfloat16


def across(a, b):
    return lax.dot_general(a, b, (((1,), (1,)), ((), ())), preferred_element_type=F32)


def along(a, b):
    return lax.dot_general(a, b, (((0,), (0,)), ((), ())), preferred_element_type=F32)


def times(a, b):
    return jnp.dot(a, b, preferred_element_type=F32)


def first_columns(place, blocks, hop, flip):
    block = lax.rem(place[0] // 2 + (blocks * HOPS - hop), blocks)
    side = place[0] % 2
    return 2 * block + (1 - side if flip else side)


def tile_copies(first, x_hbm, m_hbm, tile, mask, sems):
    width = tile.shape[1] // 2
    copies = []
    for order, column in enumerate((first, first + 1 - 2 * (first % 2))):
        source = pl.ds(pl.multiple_of(column * width, width), width)
        target = pl.ds(order * width, width)
        for i, (whole, part) in enumerate(((x_hbm, tile), (m_hbm, mask))):
            copies.append(
                pltpu.make_async_copy(whole.at[:, source], part.at[:, target], sems.at[2 * order + i])
            )
    return copies


def residue(tile, mask, predicted):
    return (mask * (tile - predicted)).astype(HALF)


def visit(steps, cells, loci, tile, mask, u1, v1_half, r2, v2, fetch=lambda: None):
    cell_half, locus_half = cells.astype(HALF), loci.astype(HALF)
    predicted = across(locus_half, cell_half)
    fetch()
    r = residue(tile[...], mask[...], predicted)
    loci = loci + steps[1] * times(r, cell_half)
    grad_cells = along(r, locus_half)
    locus_half = loci.astype(HALF)
    v1_half[...] = locus_half
    cells = cells + steps[0] * grad_cells
    u1[...] = cells
    cell_half = cells.astype(HALF)
    rows = v2[0].shape[0]
    r = residue(tile[:rows], mask[:rows], across(locus_half[:rows], cell_half))
    r2[...] = r
    v2[0][...] = loci[:rows] + steps[1] * times(r, cell_half)
    for v1 in v2[1:]:
        v1[...] = loci[rows:]


def rest_body(steps, u1, v1_half, v1, tile, mask, r2, v2):
    rows = v1.shape[0]
    cell_half = u1[...].astype(HALF)
    r = residue(tile[rows:], mask[rows:], across(v1_half[rows:], cell_half))
    r2[...] = r
    v2[...] = v1[...] + steps[1] * times(r, cell_half)


def start_body(steps, blocks, place, x_hbm, m_hbm, u_hbm, v_hbm, u1, v1_half, r2, v2, tile, mask, x, m, u, v, sems):
    rows = v.shape[0] // 2
    side = place[0] % 2
    copies = tile_copies(first_columns(place, blocks, 0, False), x_hbm, m_hbm, x, m, sems)
    inputs = [pltpu.make_async_copy(u_hbm, u, sems.at[4])]
    for order, index in enumerate((side, 1 - side)):
        source = pl.ds(pl.multiple_of(index * rows, rows), rows)
        target = pl.ds(order * rows, rows)
        inputs.append(pltpu.make_async_copy(v_hbm.at[source], v.at[target], sems.at[5 + order]))
    for copy in inputs + copies:
        copy.start()

    def fetch():
        for copy in copies:
            copy.wait()
        tile[...] = x[...].astype(F32).T
        mask[...] = m[...].astype(F32).T

    for copy in inputs:
        copy.wait()
    visit(steps, u[...], v[...], tile, mask, u1, v1_half, r2, (v2,), fetch)


def visit_body(steps, parts, u, *refs):
    loci = jnp.concatenate([part[...] for part in refs[:parts]], 0)
    tile, mask, u1, v1_half, r2, *v2 = refs[parts:]
    visit(steps, u[...], loci, tile, mask, u1, v1_half, r2, v2)


def settle(steps, u1, v1_half, residues, u2):
    r2 = residues[0][...] if len(residues) == 1 else jnp.concatenate([r[...] for r in residues], 0)
    u2[...] = u1[...] + steps[0] * along(r2, v1_half[...])


def settle_body(steps, blocks, hop, flip, place, u1, v1_half, *refs):
    *residues, x_hbm, m_hbm, u2, tile, mask, x, m, sems = refs
    copies = tile_copies(first_columns(place, blocks, hop, flip), x_hbm, m_hbm, x, m, sems)
    for copy in copies:
        copy.start()
    settle(steps, u1, v1_half, residues, u2)
    for copy in copies:
        copy.wait()
    tile[...] = x[...].astype(F32).T
    mask[...] = m[...].astype(F32).T


def finish_body(steps, u1, v1_half, *refs):
    *residues, u2 = refs
    settle(steps, u1, v1_half, residues, u2)


def store_body(other, place, half, *refs):
    *_, out, sems = refs
    rows = half.shape[0]
    index = 1 - place[0] % 2 if other else place[0] % 2
    target = pl.ds(pl.multiple_of(index * rows, rows), rows)
    copy = pltpu.make_async_copy(half, out.at[target], sems.at[0])
    copy.start()
    copy.wait()


def call(body, args, spaces, outs, scratch=(), flops=0, made=pltpu.VMEM, aliases=None):
    kinds = {"v": pltpu.VMEM, "h": pltpu.HBM, "s": pltpu.SMEM}
    placed = [
        a if s == "s" else pltpu.with_memory_space_constraint(a, kinds[s])
        for a, s in zip(args, spaces)
    ]
    return pl.pallas_call(
        body,
        out_shape=[jax.ShapeDtypeStruct(shape, dtype) for shape, dtype in outs],
        in_specs=[pl.BlockSpec(memory_space=kinds[s]) for s in spaces],
        out_specs=[pl.BlockSpec(memory_space=made) for _ in outs],
        scratch_shapes=list(scratch),
        input_output_aliases=aliases or {},
        compiler_params=pltpu.CompilerParams(vmem_limit_bytes=12 << 20),
        cost_estimate=pl.CostEstimate(flops=flops, bytes_accessed=4 << 20, transcendentals=0),
    )(*placed)


def moved(block, blocks, groups, distance, flip=0):
    route = [
        (b * groups + g, (b + distance) % blocks * groups + (g ^ flip))
        for b in range(blocks)
        for g in range(groups)
    ]
    return lax.ppermute(block, AXES, route)


def average(part_a, part_b, pending, blocks, groups, distance):
    member = lax.axis_index("group")
    bits = [1 << i for i in range(1, groups.bit_length() - 1)]
    share = part_b + moved(part_a, blocks, groups, 0, 1)
    for bit in bits:
        rows = share.shape[0] // 2
        upper = (member & bit) != 0
        low, high = share[:rows], share[rows:]
        received = moved(jnp.where(upper, low, high), blocks, groups, 0, bit)
        received, *pending = lax.optimization_barrier((received, *pending))
        share = jnp.where(upper, high, low) + received
    share = share / groups
    for place, bit in enumerate(reversed(bits)):
        upper = (member & bit) != 0
        if place == 0:
            mine = moved(share, blocks, groups, distance)
            other = moved(share, blocks, groups, distance, bit)
        else:
            mine = share
            other = moved(share, blocks, groups, 0, bit)
        share = jnp.where(
            upper, jnp.concatenate([other, mine], 0), jnp.concatenate([mine, other], 0)
        )
    return share, moved(share, blocks, groups, 0, 1), pending


def solution(mesh):
    blocks, groups = mesh.shape["blk"], mesh.shape["group"]

    def on_device(expression, observed, cell_factors, locus_factors):
        position = lax.axis_index("blk")
        side = lax.axis_index("group") % 2
        cells, rank = cell_factors.shape
        loci = locus_factors.shape[0]
        steps = (2.0 / (loci + rank), 2.0 / (cells + rank))
        work = 2 * cells * loci * rank
        place = (2 * position + side).reshape(1).astype(jnp.int32)
        wide, tall, turned = ((cells, rank), F32), ((loci, rank), F32), ((loci, cells), F32)
        part = ((loci // 2, rank), F32)
        state = [wide, ((loci, rank), HALF), ((loci, cells), HALF)]
        fetched = [pltpu.VMEM((cells, loci), HALF), pltpu.VMEM((cells, loci), jnp.int32)]

        for hop in range(HOPS):
            averaged = (hop + 1) % (HOPS // 2) == 0
            if hop == 0:
                u1, v1_half, r2, v2 = call(
                    functools.partial(start_body, steps, blocks),
                    (place, expression, observed, cell_factors, locus_factors),
                    "shhhh",
                    state + [tall],
                    [
                        pltpu.VMEM(turned[0], F32),
                        pltpu.VMEM(turned[0], F32),
                        *fetched,
                        pltpu.VMEM(wide[0], F32),
                        pltpu.VMEM(tall[0], F32),
                        pltpu.SemaphoreType.DMA((7,)),
                    ],
                    5 * work,
                )
                v2 = [v2]
            else:
                if averaged:
                    state = [wide, ((loci, rank), HALF), ((loci // 2, cells), HALF)]
                else:
                    state = [wide, ((loci, rank), HALF), ((loci, cells), HALF)]
                u1, v1_half, r2, *v2 = call(
                    functools.partial(visit_body, steps, len(parts)),
                    (u, *parts, tile, mask),
                    "v" * (3 + len(parts)),
                    state + ([part, part] if averaged else [tall]),
                    (),
                    5 * work,
                )
            residues = [r2]
            if averaged:
                va2, vb1 = v2
                r2b, vb2 = call(
                    functools.partial(rest_body, steps),
                    (u1, v1_half, vb1, tile, mask),
                    "vvvvv",
                    [((loci // 2, cells), HALF), part],
                    (),
                    work,
                )
                v2 = [va2, vb2]
                residues = [r2, r2b]
            if hop < HOPS - 1:
                u, tile, mask = call(
                    functools.partial(settle_body, steps, blocks, hop + 1, hop + 1 >= HOPS // 2),
                    (place, u1, v1_half, *residues, expression, observed),
                    "svv" + "v" * len(residues) + "hh",
                    [wide, turned, turned],
                    fetched + [pltpu.SemaphoreType.DMA((4,))],
                    work,
                )
                pending = (u, tile, mask)
            else:
                pending = call(functools.partial(finish_body, steps), (u1, v1_half, *residues), "vvvv", [wide], (), work)
            if averaged:
                distance = 1 if hop < HOPS - 1 else 1 - HOPS
                *parts, pending = average(*v2, pending, blocks, groups, distance)
                u, *rest = pending
                if rest:
                    tile, mask = rest
            else:
                parts = [moved(v2[0], blocks, groups, 1)]
        one = [pltpu.SemaphoreType.DMA((1,))]
        (whole,) = call(
            functools.partial(store_body, False), (place, parts[0]), "sv", [tall], one, made=pltpu.HBM
        )
        (whole,) = call(
            functools.partial(store_body, True), (place, parts[1], whole), "svh", [tall], one, made=pltpu.HBM, aliases={2: 0}
        )
        return u, whole

    split = P(AXES, None)
    return jax.shard_map(
        on_device,
        mesh=mesh,
        in_specs=(split, split, split, P("blk", None)),
        out_specs=(split, P("blk", None)),
        check_vma=False,
    )
```

```python
import functools

import jax
import jax.numpy as jnp
from jax import lax
from jax.experimental import pallas as pl
from jax.experimental.pallas import tpu as pltpu
from jax.sharding import PartitionSpec as P

HOPS = 6
AXES = ("blk", "group")
F32, HALF = jnp.float32, jnp.bfloat16


def across(a, b):
    return lax.dot_general(a, b, (((1,), (1,)), ((), ())), preferred_element_type=F32)


def along(a, b):
    return lax.dot_general(a, b, (((0,), (0,)), ((), ())), preferred_element_type=F32)


def times(a, b):
    return jnp.dot(a, b, preferred_element_type=F32)


def first_columns(place, blocks, hop, flip):
    block = lax.rem(place[0] // 2 + (blocks * HOPS - hop), blocks)
    side = place[0] % 2
    return 2 * block + (1 - side if flip else side)


def tile_copies(first, x_hbm, m_hbm, tile, mask, sems):
    width = tile.shape[1] // 2
    copies = []
    for order, column in enumerate((first, first + 1 - 2 * (first % 2))):
        source = pl.ds(pl.multiple_of(column * width, width), width)
        target = pl.ds(order * width, width)
        for i, (whole, part) in enumerate(((x_hbm, tile), (m_hbm, mask))):
            copies.append(
                pltpu.make_async_copy(whole.at[:, source], part.at[:, target], sems.at[2 * order + i])
            )
    return copies


def residue(tile, mask, predicted):
    return (mask * (tile - predicted)).astype(HALF)


def visit(steps, cells, loci, tile, mask, u1, v1_half, r2, v2, fetch=lambda: None):
    cell_half, locus_half = cells.astype(HALF), loci.astype(HALF)
    predicted = across(locus_half, cell_half)
    fetch()
    r = residue(tile[...], mask[...], predicted)
    loci = loci + steps[1] * times(r, cell_half)
    grad_cells = along(r, locus_half)
    locus_half = loci.astype(HALF)
    v1_half[...] = locus_half
    cells = cells + steps[0] * grad_cells
    u1[...] = cells
    cell_half = cells.astype(HALF)
    rows = v2[0].shape[0]
    r = residue(tile[:rows], mask[:rows], across(locus_half[:rows], cell_half))
    r2[...] = r
    v2[0][...] = loci[:rows] + steps[1] * times(r, cell_half)
    for v1 in v2[1:]:
        v1[...] = loci[rows:]


def rest_body(steps, u1, v1_half, v1, tile, mask, r2, v2):
    rows = v1.shape[0]
    cell_half = u1[...].astype(HALF)
    r = residue(tile[rows:], mask[rows:], across(v1_half[rows:], cell_half))
    r2[...] = r
    v2[...] = v1[...] + steps[1] * times(r, cell_half)


def start_body(steps, blocks, place, x_hbm, m_hbm, u_hbm, v_hbm, u1, v1_half, r2, v2, tile, mask, x, m, u, v, sems):
    rows = v.shape[0] // 2
    side = place[0] % 2
    copies = tile_copies(first_columns(place, blocks, 0, False), x_hbm, m_hbm, x, m, sems)
    inputs = [pltpu.make_async_copy(u_hbm, u, sems.at[4])]
    for order, index in enumerate((side, 1 - side)):
        source = pl.ds(pl.multiple_of(index * rows, rows), rows)
        target = pl.ds(order * rows, rows)
        inputs.append(pltpu.make_async_copy(v_hbm.at[source], v.at[target], sems.at[5 + order]))
    for copy in inputs + copies:
        copy.start()

    def fetch():
        for copy in copies:
            copy.wait()
        tile[...] = x[...].astype(F32).T
        mask[...] = m[...].astype(F32).T

    for copy in inputs:
        copy.wait()
    visit(steps, u[...], v[...], tile, mask, u1, v1_half, r2, (v2,), fetch)


def visit_body(steps, parts, u, *refs):
    loci = jnp.concatenate([part[...] for part in refs[:parts]], 0)
    tile, mask, u1, v1_half, r2, *v2 = refs[parts:]
    visit(steps, u[...], loci, tile, mask, u1, v1_half, r2, v2)


def settle(steps, u1, v1_half, residues, u2):
    r2 = residues[0][...] if len(residues) == 1 else jnp.concatenate([r[...] for r in residues], 0)
    u2[...] = u1[...] + steps[0] * along(r2, v1_half[...])


def settle_body(steps, blocks, hop, flip, place, u1, v1_half, *refs):
    *residues, x_hbm, m_hbm, u2, tile, mask, x, m, sems = refs
    copies = tile_copies(first_columns(place, blocks, hop, flip), x_hbm, m_hbm, x, m, sems)
    for copy in copies:
        copy.start()
    settle(steps, u1, v1_half, residues, u2)
    for copy in copies:
        copy.wait()
    tile[...] = x[...].astype(F32).T
    mask[...] = m[...].astype(F32).T


def finish_body(steps, u1, v1_half, *refs):
    *residues, u2 = refs
    settle(steps, u1, v1_half, residues, u2)


def store_body(other, place, half, *refs):
    *_, out, sems = refs
    rows = half.shape[0]
    index = 1 - place[0] % 2 if other else place[0] % 2
    target = pl.ds(pl.multiple_of(index * rows, rows), rows)
    copy = pltpu.make_async_copy(half, out.at[target], sems.at[0])
    copy.start()
    copy.wait()


def call(body, args, spaces, outs, scratch=(), flops=0, made=pltpu.VMEM, aliases=None):
    kinds = {"v": pltpu.VMEM, "h": pltpu.HBM, "s": pltpu.SMEM}
    placed = [
        a if s == "s" else pltpu.with_memory_space_constraint(a, kinds[s])
        for a, s in zip(args, spaces)
    ]
    return pl.pallas_call(
        body,
        out_shape=[jax.ShapeDtypeStruct(shape, dtype) for shape, dtype in outs],
        in_specs=[pl.BlockSpec(memory_space=kinds[s]) for s in spaces],
        out_specs=[pl.BlockSpec(memory_space=made) for _ in outs],
        scratch_shapes=list(scratch),
        input_output_aliases=aliases or {},
        compiler_params=pltpu.CompilerParams(vmem_limit_bytes=12 << 20),
        cost_estimate=pl.CostEstimate(flops=flops, bytes_accessed=4 << 20, transcendentals=0),
    )(*placed)


def moved(block, blocks, groups, distance, flip=0):
    route = [
        (b * groups + g, (b + distance) % blocks * groups + (g ^ flip))
        for b in range(blocks)
        for g in range(groups)
    ]
    return lax.ppermute(block, AXES, route)


def average(part_a, part_b, pending, blocks, groups, distance):
    member = lax.axis_index("group")
    bits = [1 << i for i in range(1, groups.bit_length() - 1)]
    share = part_b + moved(part_a, blocks, groups, 0, 1)
    for bit in bits:
        rows = share.shape[0] // 2
        upper = (member & bit) != 0
        low, high = share[:rows], share[rows:]
        received = moved(jnp.where(upper, low, high), blocks, groups, 0, bit)
        received, *pending = lax.optimization_barrier((received, *pending))
        share = jnp.where(upper, high, low) + received
    share = share / groups
    pieces = [share, share]
    for place, bit in enumerate(reversed(bits)):
        upper = (member & bit) != 0
        if place == 0:
            mine = moved(share, blocks, groups, distance)
            other = moved(share, blocks, groups, distance, bit)
        else:
            mine = pieces[0]
            other = moved(pieces[0], blocks, groups, 0, bit)
        last = place == len(bits) - 1
        both = [(mine, other)]
        if last:
            both.append((moved(mine, blocks, groups, 0, 1), moved(other, blocks, groups, 0, 1)))
        pieces = [
            jnp.where(upper, jnp.concatenate([o, m], 0), jnp.concatenate([m, o], 0)) for m, o in both
        ]
    return pieces[0], pieces[1], pending


def solution(mesh):
    blocks, groups = mesh.shape["blk"], mesh.shape["group"]

    def on_device(expression, observed, cell_factors, locus_factors):
        position = lax.axis_index("blk")
        side = lax.axis_index("group") % 2
        cells, rank = cell_factors.shape
        loci = locus_factors.shape[0]
        steps = (2.0 / (loci + rank), 2.0 / (cells + rank))
        work = 2 * cells * loci * rank
        place = (2 * position + side).reshape(1).astype(jnp.int32)
        wide, tall, turned = ((cells, rank), F32), ((loci, rank), F32), ((loci, cells), F32)
        part = ((loci // 2, rank), F32)
        state = [wide, ((loci, rank), HALF), ((loci, cells), HALF)]
        fetched = [pltpu.VMEM((cells, loci), HALF), pltpu.VMEM((cells, loci), jnp.int32)]

        for hop in range(HOPS):
            averaged = (hop + 1) % (HOPS // 2) == 0
            if hop == 0:
                u1, v1_half, r2, v2 = call(
                    functools.partial(start_body, steps, blocks),
                    (place, expression, observed, cell_factors, locus_factors),
                    "shhhh",
                    state + [tall],
                    [
                        pltpu.VMEM(turned[0], F32),
                        pltpu.VMEM(turned[0], F32),
                        *fetched,
                        pltpu.VMEM(wide[0], F32),
                        pltpu.VMEM(tall[0], F32),
                        pltpu.SemaphoreType.DMA((7,)),
                    ],
                    5 * work,
                )
                v2 = [v2]
            else:
                if averaged:
                    state = [wide, ((loci, rank), HALF), ((loci // 2, cells), HALF)]
                else:
                    state = [wide, ((loci, rank), HALF), ((loci, cells), HALF)]
                u1, v1_half, r2, *v2 = call(
                    functools.partial(visit_body, steps, len(parts)),
                    (u, *parts, tile, mask),
                    "v" * (3 + len(parts)),
                    state + ([part, part] if averaged else [tall]),
                    (),
                    5 * work,
                )
            residues = [r2]
            if averaged:
                va2, vb1 = v2
                r2b, vb2 = call(
                    functools.partial(rest_body, steps),
                    (u1, v1_half, vb1, tile, mask),
                    "vvvvv",
                    [((loci // 2, cells), HALF), part],
                    (),
                    work,
                )
                v2 = [va2, vb2]
                residues = [r2, r2b]
            if hop < HOPS - 1:
                u, tile, mask = call(
                    functools.partial(settle_body, steps, blocks, hop + 1, hop + 1 >= HOPS // 2),
                    (place, u1, v1_half, *residues, expression, observed),
                    "svv" + "v" * len(residues) + "hh",
                    [wide, turned, turned],
                    fetched + [pltpu.SemaphoreType.DMA((4,))],
                    work,
                )
                pending = (u, tile, mask)
            else:
                pending = call(functools.partial(finish_body, steps), (u1, v1_half, *residues), "vvvv", [wide], (), work)
            if averaged:
                distance = 1 if hop < HOPS - 1 else 1 - HOPS
                *parts, pending = average(*v2, pending, blocks, groups, distance)
                u, *rest = pending
                if rest:
                    tile, mask = rest
            else:
                parts = [moved(v2[0], blocks, groups, 1)]
        one = [pltpu.SemaphoreType.DMA((1,))]
        (whole,) = call(
            functools.partial(store_body, False), (place, parts[0]), "sv", [tall], one, made=pltpu.HBM
        )
        (whole,) = call(
            functools.partial(store_body, True), (place, parts[1], whole), "svh", [tall], one, made=pltpu.HBM, aliases={2: 0}
        )
        return u, whole

    split = P(AXES, None)
    return jax.shard_map(
        on_device,
        mesh=mesh,
        in_specs=(split, split, split, P("blk", None)),
        out_specs=(split, P("blk", None)),
        check_vma=False,
    )
```

```python
import functools

import jax
import jax.numpy as jnp
from jax import lax
from jax.experimental import pallas as pl
from jax.experimental.pallas import tpu as pltpu
from jax.sharding import PartitionSpec as P

HOPS = 6
AXES = ("blk", "group")
F32, HALF = jnp.float32, jnp.bfloat16


def across(a, b):
    return lax.dot_general(a, b, (((1,), (1,)), ((), ())), preferred_element_type=F32)


def along(a, b):
    return lax.dot_general(a, b, (((0,), (0,)), ((), ())), preferred_element_type=F32)


def times(a, b):
    return jnp.dot(a, b, preferred_element_type=F32)


def first_columns(place, blocks, hop, flip):
    block = lax.rem(place[0] // 2 + (blocks * HOPS - hop), blocks)
    side = place[0] % 2
    return 2 * block + (1 - side if flip else side)


def tile_copies(first, x_hbm, m_hbm, tile, mask, sems):
    width = tile.shape[1] // 2
    copies = []
    for order, column in enumerate((first, first + 1 - 2 * (first % 2))):
        source = pl.ds(pl.multiple_of(column * width, width), width)
        target = pl.ds(order * width, width)
        for i, (whole, part) in enumerate(((x_hbm, tile), (m_hbm, mask))):
            copies.append(
                pltpu.make_async_copy(whole.at[:, source], part.at[:, target], sems.at[2 * order + i])
            )
    return copies


def residue(tile, mask, predicted):
    return (mask * (tile - predicted)).astype(HALF)


def visit(steps, cells, loci, tile, mask, u1, v1_half, r2, v2, fetch=lambda: None):
    cell_half, locus_half = cells.astype(HALF), loci.astype(HALF)
    predicted = across(locus_half, cell_half)
    fetch()
    r = residue(tile[...], mask[...], predicted)
    loci = loci + steps[1] * times(r, cell_half)
    grad_cells = along(r, locus_half)
    locus_half = loci.astype(HALF)
    v1_half[...] = locus_half
    cells = cells + steps[0] * grad_cells
    u1[...] = cells
    cell_half = cells.astype(HALF)
    rows = v2[0].shape[0]
    r = residue(tile[:rows], mask[:rows], across(locus_half[:rows], cell_half))
    r2[...] = r
    v2[0][...] = loci[:rows] + steps[1] * times(r, cell_half)
    for v1 in v2[1:]:
        v1[...] = loci[rows:]


def rest_body(steps, u1, v1_half, v1, tile, mask, r2, v2):
    rows = v1.shape[0]
    cell_half = u1[...].astype(HALF)
    r = residue(tile[rows:], mask[rows:], across(v1_half[rows:], cell_half))
    r2[...] = r
    v2[...] = v1[...] + steps[1] * times(r, cell_half)


def start_body(steps, blocks, place, x_hbm, m_hbm, u_hbm, v_hbm, u1, v1_half, r2, v2, tile, mask, x, m, u, v, sems):
    rows = v.shape[0] // 2
    side = place[0] % 2
    copies = tile_copies(first_columns(place, blocks, 0, False), x_hbm, m_hbm, x, m, sems)
    inputs = [pltpu.make_async_copy(u_hbm, u, sems.at[4])]
    for order, index in enumerate((side, 1 - side)):
        source = pl.ds(pl.multiple_of(index * rows, rows), rows)
        target = pl.ds(order * rows, rows)
        inputs.append(pltpu.make_async_copy(v_hbm.at[source], v.at[target], sems.at[5 + order]))
    for copy in inputs + copies:
        copy.start()

    def fetch():
        for copy in copies:
            copy.wait()
        tile[...] = x[...].astype(F32).T
        mask[...] = m[...].astype(F32).T

    for copy in inputs:
        copy.wait()
    visit(steps, u[...], v[...], tile, mask, u1, v1_half, r2, (v2,), fetch)


def visit_body(steps, parts, u, *refs):
    loci = jnp.concatenate([part[...] for part in refs[:parts]], 0)
    tile, mask, u1, v1_half, r2, *v2 = refs[parts:]
    visit(steps, u[...], loci, tile, mask, u1, v1_half, r2, v2)


def settle(steps, u1, v1_half, residues, u2):
    r2 = residues[0][...] if len(residues) == 1 else jnp.concatenate([r[...] for r in residues], 0)
    u2[...] = u1[...] + steps[0] * along(r2, v1_half[...])


def settle_body(steps, blocks, hop, flip, place, u1, v1_half, *refs):
    *residues, x_hbm, m_hbm, u2, tile, mask, x, m, sems = refs
    copies = tile_copies(first_columns(place, blocks, hop, flip), x_hbm, m_hbm, x, m, sems)
    for copy in copies:
        copy.start()
    settle(steps, u1, v1_half, residues, u2)
    for copy in copies:
        copy.wait()
    tile[...] = x[...].astype(F32).T
    mask[...] = m[...].astype(F32).T


def finish_body(steps, u1, v1_half, *refs):
    *residues, u2 = refs
    settle(steps, u1, v1_half, residues, u2)


def store_body(other, place, half, *refs):
    *_, out, sems = refs
    rows = half.shape[0]
    index = 1 - place[0] % 2 if other else place[0] % 2
    target = pl.ds(pl.multiple_of(index * rows, rows), rows)
    copy = pltpu.make_async_copy(half, out.at[target], sems.at[0])
    copy.start()
    copy.wait()


def call(body, args, spaces, outs, scratch=(), flops=0, made=pltpu.VMEM, aliases=None):
    kinds = {"v": pltpu.VMEM, "h": pltpu.HBM, "s": pltpu.SMEM}
    placed = [
        a if s == "s" else pltpu.with_memory_space_constraint(a, kinds[s])
        for a, s in zip(args, spaces)
    ]
    return pl.pallas_call(
        body,
        out_shape=[jax.ShapeDtypeStruct(shape, dtype) for shape, dtype in outs],
        in_specs=[pl.BlockSpec(memory_space=kinds[s]) for s in spaces],
        out_specs=[pl.BlockSpec(memory_space=made) for _ in outs],
        scratch_shapes=list(scratch),
        input_output_aliases=aliases or {},
        compiler_params=pltpu.CompilerParams(vmem_limit_bytes=12 << 20),
        cost_estimate=pl.CostEstimate(flops=flops, bytes_accessed=4 << 20, transcendentals=0),
    )(*placed)


def moved(block, blocks, groups, distance, flip=0):
    route = [
        (b * groups + g, (b + distance) % blocks * groups + (g ^ flip))
        for b in range(blocks)
        for g in range(groups)
    ]
    return lax.ppermute(block, AXES, route)


def average(part_a, part_b, pending, blocks, groups, distance):
    member = lax.axis_index("group")
    bits = [1 << i for i in range(1, groups.bit_length() - 1)]
    share = None
    for bit in bits:
        upper = (member & bit) != 0
        rows = (part_b if share is None else share).shape[0] // 2

        def split(block):
            low, high = block[:rows], block[rows:]
            return jnp.where(upper, low, high), jnp.where(upper, high, low)

        if share is None:
            send, keep = (b + moved(a, blocks, groups, 0, 1) for a, b in zip(split(part_a), split(part_b)))
        else:
            send, keep = split(share)
        received = moved(send, blocks, groups, 0, bit)
        received, *pending = lax.optimization_barrier((received, *pending))
        share = keep + received
    share = share / groups
    pieces = [share, share]
    for place, bit in enumerate(reversed(bits)):
        upper = (member & bit) != 0
        if place == 0:
            mine = moved(share, blocks, groups, distance)
            other = moved(share, blocks, groups, distance, bit)
        else:
            mine = pieces[0]
            other = moved(pieces[0], blocks, groups, 0, bit)
        last = place == len(bits) - 1
        both = [(mine, other)]
        if last:
            both.append((moved(mine, blocks, groups, 0, 1), moved(other, blocks, groups, 0, 1)))
        pieces = [
            jnp.where(upper, jnp.concatenate([o, m], 0), jnp.concatenate([m, o], 0)) for m, o in both
        ]
    return pieces[0], pieces[1], pending


def solution(mesh):
    blocks, groups = mesh.shape["blk"], mesh.shape["group"]

    def on_device(expression, observed, cell_factors, locus_factors):
        position = lax.axis_index("blk")
        side = lax.axis_index("group") % 2
        cells, rank = cell_factors.shape
        loci = locus_factors.shape[0]
        steps = (2.0 / (loci + rank), 2.0 / (cells + rank))
        work = 2 * cells * loci * rank
        place = (2 * position + side).reshape(1).astype(jnp.int32)
        wide, tall, turned = ((cells, rank), F32), ((loci, rank), F32), ((loci, cells), F32)
        part = ((loci // 2, rank), F32)
        state = [wide, ((loci, rank), HALF), ((loci, cells), HALF)]
        fetched = [pltpu.VMEM((cells, loci), HALF), pltpu.VMEM((cells, loci), jnp.int32)]

        for hop in range(HOPS):
            averaged = (hop + 1) % (HOPS // 2) == 0
            if hop == 0:
                u1, v1_half, r2, v2 = call(
                    functools.partial(start_body, steps, blocks),
                    (place, expression, observed, cell_factors, locus_factors),
                    "shhhh",
                    state + [tall],
                    [
                        pltpu.VMEM(turned[0], F32),
                        pltpu.VMEM(turned[0], F32),
                        *fetched,
                        pltpu.VMEM(wide[0], F32),
                        pltpu.VMEM(tall[0], F32),
                        pltpu.SemaphoreType.DMA((7,)),
                    ],
                    5 * work,
                )
                v2 = [v2]
            else:
                if averaged:
                    state = [wide, ((loci, rank), HALF), ((loci // 2, cells), HALF)]
                else:
                    state = [wide, ((loci, rank), HALF), ((loci, cells), HALF)]
                u1, v1_half, r2, *v2 = call(
                    functools.partial(visit_body, steps, len(parts)),
                    (u, *parts, tile, mask),
                    "v" * (3 + len(parts)),
                    state + ([part, part] if averaged else [tall]),
                    (),
                    5 * work,
                )
            residues = [r2]
            if averaged:
                va2, vb1 = v2
                r2b, vb2 = call(
                    functools.partial(rest_body, steps),
                    (u1, v1_half, vb1, tile, mask),
                    "vvvvv",
                    [((loci // 2, cells), HALF), part],
                    (),
                    work,
                )
                v2 = [va2, vb2]
                residues = [r2, r2b]
            if hop < HOPS - 1:
                u, tile, mask = call(
                    functools.partial(settle_body, steps, blocks, hop + 1, hop + 1 >= HOPS // 2),
                    (place, u1, v1_half, *residues, expression, observed),
                    "svv" + "v" * len(residues) + "hh",
                    [wide, turned, turned],
                    fetched + [pltpu.SemaphoreType.DMA((4,))],
                    work,
                )
                pending = (u, tile, mask)
            else:
                pending = call(functools.partial(finish_body, steps), (u1, v1_half, *residues), "vvvv", [wide], (), work)
            if averaged:
                distance = 1 if hop < HOPS - 1 else 1 - HOPS
                *parts, pending = average(*v2, pending, blocks, groups, distance)
                u, *rest = pending
                if rest:
                    tile, mask = rest
            else:
                parts = [moved(v2[0], blocks, groups, 1)]
        one = [pltpu.SemaphoreType.DMA((1,))]
        (whole,) = call(
            functools.partial(store_body, False), (place, parts[0]), "sv", [tall], one, made=pltpu.HBM
        )
        (whole,) = call(
            functools.partial(store_body, True), (place, parts[1], whole), "svh", [tall], one, made=pltpu.HBM, aliases={2: 0}
        )
        return u, whole

    split = P(AXES, None)
    return jax.shard_map(
        on_device,
        mesh=mesh,
        in_specs=(split, split, split, P("blk", None)),
        out_specs=(split, P("blk", None)),
        check_vma=False,
    )
```
